256 devices in a mesh: xfer: 8 (over z), row: 8 (over y_hi, x), col: 4 (over y_lo, core).
Axes of the slice: x: 4, y: 4 (y_hi: 2, y_lo: 2; y = y_hi * 2 + y_lo), z: 8, core: 2. Of those that a mesh axis runs over, the one named last changes fastest.
Arguments:
- vertex: bfloat16 [8, 2, 3584, 3584], P('xfer', None, 'row', 'col'), may hold values from -6 to 6
- bubble: bfloat16 [8, 2, 3584], P('xfer', None, 'row'), may hold values from -0.0625 to 0.0625
- previous: bfloat16 [8, 2, 3584, 3584], P('xfer', None, 'row', 'col'), may hold values from -6 to 6
- cross_map: int32 [8, 64], replicated, may hold values from 0 to 7, as said below
Outputs:
- updated: bfloat16 [8, 2, 3584, 3584], P('xfer', None, 'row', 'col')
- crossed: bfloat16 [8, 2, 3584, 3584], P('xfer', None, 'row', 'col')
The draws below stay inside these ranges and needn't reach their ends.
Inputs may be any that keep to these rules, and one draw needn't show every extreme that they name: For every block b, cross_map[:, b] names each of the 8 transfers once; for every transfer q and every r, the 8 entries cross_map[q, r * 8] to cross_map[q, r * 8 + 7] name each transfer once.
All inputs are finite; a program needn't handle non-finite values.
Results may differ from the reference program's by a relative error of at most 0.0044.
Values may be sent and summed in bfloat16 or wider, within the bound.
A program may use at most 128 MiB of HBM per device.

```python
import jax
import jax.numpy as jnp

M = 3584
TRANSFERS = 8
BLOCKS = 64


def draw_cross_map(key, part):
    key = jax.random.fold_in(key, 7)
    keys = jax.random.split(key, 3)
    odd_first = 2 * jax.random.randint(keys[0], (), 0, max(TRANSFERS // 2, 1)) + 1
    odd_second = 2 * jax.random.randint(keys[1], (), 0, max(TRANSFERS // 2, 1)) + 1
    offsets = jax.random.randint(keys[2], (BLOCKS // TRANSFERS,), 0, TRANSFERS)
    target = jnp.arange(TRANSFERS, dtype=jnp.int32)[:, None]
    blocks = jnp.arange(BLOCKS, dtype=jnp.int32)[None, :]
    within = blocks % TRANSFERS
    outer = blocks // TRANSFERS
    return ((target * odd_first + within * odd_second + offsets[outer]) % TRANSFERS).astype(jnp.int32)


def block_levels(stream_key, shape, cuts, smallest, high):
    def one(position, shards_of):
        heights = jax.random.uniform(jax.random.fold_in(jax.random.fold_in(stream_key, 6), position), (shards_of,), jnp.float32, smallest / len(cuts), high / len(cuts))
        return jnp.repeat(jnp.exp(heights), shape[position] // shards_of).reshape((-1,) + (1,) * (len(shape) - position - 1))

    factor_of = one(*cuts[0])
    for cut in cuts[1:]:
        factor_of = factor_of * one(*cut)
    return factor_of


def centred(own_key, dims, spread, limit, pieces=(), held_as=jnp.bfloat16):
    loudness = block_levels(own_key, dims, pieces, -0.22, 0.18) if pieces else 1.0
    result = jax.random.normal(own_key, dims, jnp.float32) * spread * loudness
    return jnp.minimum(jnp.maximum(result, -limit), limit).astype(held_as)


def setup_inputs(seed: int = 0) -> dict:
    arg_keys = jax.random.split(jax.random.key(seed), 5)
    vertex = centred(arg_keys[0], (TRANSFERS, 2, M, M), 1.0, 6.0, ((0, 8), (2, 8), (3, 4)))
    bubble = centred(arg_keys[1], (TRANSFERS, 2, M), (2 * M) ** -0.5, 0.0625, ((0, 8), (2, 8)))
    previous = centred(arg_keys[2], (TRANSFERS, 2, M, M), 1.0, 6.0, ((0, 8), (2, 8), (3, 4)))
    cross_map = draw_cross_map(jax.random.fold_in(arg_keys[4], 71), 0)
    return {"vertex": vertex, "bubble": bubble, "previous": previous, "cross_map": cross_map}


def complex_product(left, right):
    size = left.shape[1]
    stacked = left.reshape(2 * size, left.shape[2])
    joined = jnp.concatenate([right[0], right[1]], axis=1)
    total = jnp.dot(stacked, joined, preferred_element_type=jnp.float32)
    width = right.shape[2]
    real = total[:size, :width] - total[size:, width:]
    imag = total[:size, width:] + total[size:, :width]
    return jnp.stack([real, imag])


def reference(vertex, bubble, previous, cross_map):
    results = []
    for index in range(TRANSFERS):
        diag = bubble[index].astype(jnp.float32)
        prev = previous[index].astype(jnp.float32)
        first = diag[0][:, None]
        second = diag[1][:, None]
        bubbled = jnp.stack([first * prev[0] - second * prev[1], first * prev[1] + second * prev[0]]).astype(jnp.bfloat16)
        product = complex_product(vertex[index], bubbled)
        results.append((vertex[index].astype(jnp.float32) + product).astype(jnp.bfloat16))
    updated = jnp.stack(results)
    height = M // BLOCKS
    blocked = updated.reshape(TRANSFERS, 2, BLOCKS, height, M)
    picked = blocked[cross_map, :, jnp.arange(BLOCKS, dtype=jnp.int32)[None, :]]
    crossed = jnp.transpose(picked, (0, 2, 1, 3, 4)).reshape(TRANSFERS, 2, M, M)
    return updated, crossed
```

```python
import jax
import jax.numpy as jnp
from jax import lax
from jax.experimental import pallas as pl
from jax.experimental.pallas import tpu as pltpu
from jax.sharding import PartitionSpec as P

MESH = pl.DeviceIdType.MESH
CHUNKS = 7
W = 128
H = 448
D = 896
G = 8
T = 56
LAG = 2
LATE = 4
BF = jnp.bfloat16
F32 = jnp.float32


def kernel(
    vertex,
    bubble,
    previous,
    cmap,
    updated,
    crossed,
    panel,
    prev,
    bub,
    kept,
    part_out,
    part_in,
    turn,
    settled,
    cross_out,
    cross_in,
    load_sem,
    t1_s,
    t1_r,
    t2_s,
    t2_r,
    d1_s,
    d1_r,
    d2_s,
    d2_r,
    bx_s,
    bx_r,
    by_s,
    by_r,
    c_s,
    c_r,
    z_s,
    z_r,
):
    z = lax.axis_index("xfer")
    row = lax.axis_index("row")
    col = lax.axis_index("col")
    x = lax.rem(row, 4)
    yh = lax.div(row, 4)
    yl = lax.div(col, 2)
    core = lax.rem(col, 2)
    other = 1 - yh
    right = (z, yh * 4 + lax.rem(x + 1, 4), col)
    left = (z, yh * 4 + lax.rem(x + 3, 4), col)
    beside = (z, row, (1 - yl) * 2 + core)
    across = (z, other * 4 + x, (1 - yl) * 2 + core)
    sibling = (z, row, yl * 2 + 1 - core)
    partner = (z, other * 4 + x, col)
    own = jnp.where(yh == yl, yh, 2)

    def remote(src, dst, send, recv, device):
        return pltpu.make_async_remote_copy(
            src_ref=src, dst_ref=dst, send_sem=send, recv_sem=recv, device_id=device, device_id_type=MESH
        )

    load_a = pltpu.make_async_copy(vertex, panel.at[core, own], load_sem.at[0])
    load_p = pltpu.make_async_copy(previous, prev, load_sem.at[1])
    load_a.start()
    load_p.start()

    barrier = pltpu.get_barrier_semaphore()
    for device in (right, left, beside, across, sibling, partner):
        pl.semaphore_signal(barrier, inc=1, device_id=device, device_id_type=MESH)
    for step in range(1, G):
        pl.semaphore_signal(barrier, inc=1, device_id=(lax.rem(z + step, G), row, col), device_id_type=MESH)
    pl.semaphore_wait(barrier, 6 + G - 1)

    def t1(i):
        ref = panel.at[core, own, pl.ds(pl.multiple_of(i * W, W), W)]
        return remote(ref, ref, t1_s.at[i], t1_r.at[i], beside)

    def t1_arrives(i):
        slot = jnp.where(yh == yl, 2, yh)
        ref = panel.at[core, slot, pl.ds(pl.multiple_of(i * W, W), W)]
        return remote(ref, ref, t1_s.at[i], t1_r.at[i], beside)

    def t2(i):
        rows = pl.ds(pl.multiple_of(i * W, W), W)
        return remote(panel.at[core, 2, rows], panel.at[core, yh, rows], t2_s.at[i], t2_r.at[i], across)

    def t2_arrives(i):
        ref = panel.at[core, other, pl.ds(pl.multiple_of(i * W, W), W)]
        return remote(ref, ref, t2_s.at[i], t2_r.at[i], across)

    def d1(which):
        return remote(panel.at[which, yh], panel.at[which, yh], d1_s.at[0], d1_r.at[0], sibling)

    def d2(which, i):
        ref = panel.at[which, other, pl.ds(pl.multiple_of(i * W, W), W)]
        return remote(ref, ref, d2_s.at[i], d2_r.at[i], sibling)

    def bx(n, way):
        ref = bub.at[n, pl.ds(pl.multiple_of(x * H, H), H)]
        return remote(ref, ref, bx_s.at[way, n], bx_r.at[way, n], (right, left)[way])

    def bx_arrives(n, way):
        ref = bub.at[n, pl.ds(pl.multiple_of(lax.rem(x + (3, 1)[way], 4) * H, H), H)]
        return remote(ref, ref, bx_s.at[way, n], bx_r.at[way, n], (right, left)[way])

    def by(n, way):
        start = lax.rem(x + (3, 1)[way], 4) * H + way * (H // 2)
        ref = bub.at[n, pl.ds(pl.multiple_of(start, H // 2), H // 2)]
        return remote(ref, ref, by_s.at[way, n], by_r.at[way, n], (right, left)[way])

    def by_arrives(n, way):
        start = lax.rem(x + 2, 4) * H + way * (H // 2)
        ref = bub.at[n, pl.ds(pl.multiple_of(start, H // 2), H // 2)]
        return remote(ref, ref, by_s.at[way, n], by_r.at[way, n], (right, left)[way])

    def c(n):
        return remote(part_out.at[n], part_in.at[n], c_s.at[n], c_r.at[n], partner)

    def cross(n, step):
        device = (lax.rem(z + step, G), row, col)
        return remote(cross_out.at[n, step], cross_in.at[n, step], z_s.at[n, step], z_r.at[n, step], device)

    def loop(count, body):
        def run(i, carry):
            body(i)
            return carry

        lax.fori_loop(0, count, run, 0)

    load_a.wait()
    loop(CHUNKS, lambda i: t1(i).start())

    load_p.wait()
    diag = bubble[...].astype(F32)
    first = jnp.broadcast_to(diag[0:1, :], (W, H)).T
    second = jnp.broadcast_to(diag[1:2, :], (W, H)).T

    def make_bubbled(n):
        columns = pl.ds(pl.multiple_of(n * W, W), W)
        real = prev[pl.ds(0, H), columns].astype(F32)
        imag = prev[pl.ds(H, H), columns].astype(F32)
        rows = pl.ds(pl.multiple_of(x * H, H), H)
        bub[n, rows, pl.ds(0, W)] = (first * real - second * imag).astype(BF)
        bub[n, rows, pl.ds(W, W)] = (first * imag + second * real).astype(BF)
        bx(n, 0).start()
        bx(n, 1).start()

    loop(CHUNKS, make_bubbled)

    def relay(i):
        t1_arrives(i).wait_recv()
        t2(i).start()
        for way in (0, 1):
            bx_arrives(i, way).wait_recv()
            by(i, way).start()

    loop(CHUNKS, relay)
    d1(core).start()

    def share(i):
        t2_arrives(i).wait_recv()
        d2(core, i).start()

    loop(CHUNKS, share)
    d1(1 - core).wait_recv()
    loop(CHUNKS, lambda i: d2(1 - core, i).wait_recv())

    goes = []
    for step in range(G):
        target = lax.rem(z + step, G)
        index = jnp.int32(0)
        for block in range(G):
            index = jnp.where(cmap[target, row * G + block] == z, block, index)
        goes.append(index)
    comes = []
    for block in range(G):
        back = z - cmap[z, row * G + block]
        comes.append(jnp.where(back < 0, back + G, back))

    def product(n, slot):
        total = jnp.dot(panel[0, slot], bub[n, pl.ds(0, D)], preferred_element_type=F32)
        total = total + jnp.dot(panel[1, slot], bub[n, pl.ds(D, D)], preferred_element_type=F32)
        real = total[:H, :W] - total[H:, W:]
        imag = total[:H, W:] + total[H:, :W]
        return real, imag

    def multiply(n):
        for way in (0, 1):
            by_arrives(n, way).wait_recv()
        real, imag = product(n, other)
        part_out[n, pl.ds(0, H)] = real.astype(BF)
        part_out[n, pl.ds(H, H)] = imag.astype(BF)
        c(n).start()
        real, imag = product(n, yh)
        kept[n, pl.ds(0, H)] = real
        kept[n, pl.ds(H, H)] = imag

    def finish(n):
        c(n).wait_recv()
        columns = pl.ds(pl.multiple_of(n * W, W), W)
        value = panel[core, own, :, columns].astype(F32) + (kept[n] + part_in[n].astype(F32))
        updated[:, columns] = value.astype(BF)
        for block in range(G):
            low = value[block * T : block * T + T]
            high = value[H + block * T : H + block * T + T]
            turn[block] = jnp.concatenate([low, high], axis=0).astype(BF)
        for step in range(G):
            if step:
                cross_out[n, step] = turn[goes[step]]
                cross(n, step).start()
            else:
                cross_in[n, step] = turn[goes[step]]

    def place(n):
        for step in range(1, G):
            cross(n, step).wait_recv()
        columns = pl.ds(pl.multiple_of(n * W, W), W)
        settled[...] = cross_in[n]
        blocks = [settled[comes[block]].astype(F32) for block in range(G)]
        crossed[pl.ds(0, H), columns] = jnp.concatenate([b[:T] for b in blocks], axis=0).astype(BF)
        crossed[pl.ds(H, H), columns] = jnp.concatenate([b[T:] for b in blocks], axis=0).astype(BF)

    def step(n):
        @pl.when(n < CHUNKS)
        def _():
            multiply(n)

        @pl.when((n >= LAG) & (n < CHUNKS + LAG))
        def _():
            finish(n - LAG)

        @pl.when(n >= LATE)
        def _():
            place(n - LATE)

    loop(CHUNKS + LATE, step)

    d1(core).wait_send()

    def drain(i):
        t1(i).wait_send()
        t2(i).wait_send()
        d2(core, i).wait_send()
        for way in (0, 1):
            bx(i, way).wait_send()
            by(i, way).wait_send()
        c(i).wait_send()
        for step in range(1, G):
            cross(i, step).wait_send()

    loop(CHUNKS, drain)


def shards(vertex, bubble, previous, cross_map):
    dma = pltpu.SemaphoreType.DMA
    updated, crossed = pl.pallas_call(
        kernel,
        out_shape=[jax.ShapeDtypeStruct((D, D), BF)] * 2,
        in_specs=[
            pl.BlockSpec(memory_space=pl.ANY),
            pl.BlockSpec(memory_space=pltpu.VMEM),
            pl.BlockSpec(memory_space=pl.ANY),
            pl.BlockSpec(memory_space=pltpu.SMEM),
        ],
        out_specs=[pl.BlockSpec(memory_space=pltpu.VMEM)] * 2,
        scratch_shapes=[
            pltpu.VMEM((2, 3, D, D), BF),
            pltpu.VMEM((D, D), BF),
            pltpu.VMEM((CHUNKS, 4 * H, 2 * W), BF),
            pltpu.VMEM((CHUNKS, D, W), F32),
            pltpu.VMEM((CHUNKS, D, W), BF),
            pltpu.VMEM((CHUNKS, D, W), BF),
            pltpu.VMEM((G, 2 * T, W), BF),
            pltpu.VMEM((G, 2 * T, W), BF),
            pltpu.VMEM((CHUNKS, G, 2 * T, W), BF),
            pltpu.VMEM((CHUNKS, G, 2 * T, W), BF),
            dma((2,)),
            dma((CHUNKS,)),
            dma((CHUNKS,)),
            dma((CHUNKS,)),
            dma((CHUNKS,)),
            dma((1,)),
            dma((1,)),
            dma((CHUNKS,)),
            dma((CHUNKS,)),
            dma((2, CHUNKS)),
            dma((2, CHUNKS)),
            dma((2, CHUNKS)),
            dma((2, CHUNKS)),
            dma((CHUNKS,)),
            dma((CHUNKS,)),
            dma((CHUNKS, G)),
            dma((CHUNKS, G)),
        ],
        compiler_params=pltpu.CompilerParams(
            collective_id=0, has_side_effects=True, vmem_limit_bytes=56 * 2**20
        ),
        cost_estimate=pl.CostEstimate(flops=8 * H * 4 * D * D, bytes_accessed=8 * D * D, transcendentals=0),
    )(vertex.reshape(D, D), bubble.reshape(2, H), previous.reshape(D, D), cross_map)
    return updated.reshape(1, 2, H, D), crossed.reshape(1, 2, H, D)


def solution(mesh):
    in_specs = (
        P("xfer", None, "row", "col"),
        P("xfer", None, "row"),
        P("xfer", None, "row", "col"),
        P(),
    )
    out_specs = (P("xfer", None, "row", "col"), P("xfer", None, "row", "col"))
    return jax.shard_map(shards, mesh=mesh, in_specs=in_specs, out_specs=out_specs, check_vma=False)
```

```python
import jax
import jax.numpy as jnp
from jax import lax
from jax.experimental import pallas as pl
from jax.experimental.pallas import tpu as pltpu
from jax.sharding import PartitionSpec as P

MESH = pl.DeviceIdType.MESH
CHUNKS = 7
W = 128
H = 448
D = 896
G = 8
T = 56
AHEAD = 3
PIECES = 14
R = 64
E = 8
GROUPS = ((0, 4), (4, 3))
BF = jnp.bfloat16
F32 = jnp.float32


def kernel(
    vertex,
    bubble,
    previous,
    cross_map,
    updated_out,
    crossed_out,
    updated,
    crossed,
    panel,
    raw,
    prev,
    diag,
    cmap,
    bub,
    kept,
    part_out,
    part_in,
    turn,
    settled,
    cross_out,
    cross_in,
    load_sem,
    store_sem,
    t1_s,
    t1_r,
    t2_s,
    t2_r,
    d1_s,
    d1_r,
    d2_s,
    d2_r,
    bx_s,
    bx_r,
    by_s,
    by_r,
    c_s,
    c_r,
    z_s,
    z_r,
    go,
):
    z = lax.axis_index("xfer")
    row = lax.axis_index("row")
    col = lax.axis_index("col")
    x = lax.rem(row, 4)
    yh = lax.div(row, 4)
    yl = lax.div(col, 2)
    core = lax.rem(col, 2)
    other = 1 - yh
    right = (z, yh * 4 + lax.rem(x + 1, 4), col)
    left = (z, yh * 4 + lax.rem(x + 3, 4), col)
    beside = (z, row, (1 - yl) * 2 + core)
    across = (z, other * 4 + x, (1 - yl) * 2 + core)
    sibling = (z, row, yl * 2 + 1 - core)
    partner = (z, other * 4 + x, col)
    own = jnp.where(yh == yl, yh, 2)

    def remote(src, dst, send, recv, device):
        return pltpu.make_async_remote_copy(
            src_ref=src, dst_ref=dst, send_sem=send, recv_sem=recv, device_id=device, device_id_type=MESH
        )

    load_a = pltpu.make_async_copy(vertex, raw, load_sem.at[0])
    load_p = pltpu.make_async_copy(previous, prev, load_sem.at[1])
    load_d = pltpu.make_async_copy(bubble, diag, load_sem.at[2])
    load_m = pltpu.make_async_copy(cross_map, cmap, load_sem.at[3])
    for load in (load_a, load_p, load_d, load_m):
        load.start()

    barrier = pltpu.get_barrier_semaphore()
    for device in (right, left, beside, across, sibling, partner):
        pl.semaphore_signal(barrier, inc=1, device_id=device, device_id_type=MESH)
    for step in range(1, G):
        pl.semaphore_signal(barrier, inc=1, device_id=(lax.rem(z + step, G), row, col), device_id_type=MESH)

    def half(which):
        return pl.ds(pl.multiple_of(which * D, D), D)

    def t1(i):
        ref = panel.at[own, pl.ds(pl.multiple_of(i * R, R), R), half(core)]
        return remote(ref, ref, t1_s.at[0], t1_r.at[i], beside)

    def t1_arrives(i):
        slot = jnp.where(yh == yl, 2, yh)
        ref = panel.at[slot, pl.ds(pl.multiple_of(i * R, R), R), half(core)]
        return remote(ref, ref, t1_s.at[0], t1_r.at[i], beside)

    def t2(i):
        rows = pl.ds(pl.multiple_of(i * R, R), R)
        return remote(panel.at[2, rows, half(core)], panel.at[yh, rows, half(core)], t2_s.at[0], t2_r.at[i], across)

    def t2_arrives(i):
        ref = panel.at[other, pl.ds(pl.multiple_of(i * R, R), R), half(core)]
        return remote(ref, ref, t2_s.at[0], t2_r.at[i], across)

    def group_rows(group):
        first, count = GROUPS[group]
        return pl.ds(first * W, count * W)

    def d1(which, group):
        ref = panel.at[yh, group_rows(group), half(which)]
        return remote(ref, ref, d1_s.at[0], d1_r.at[group], sibling)

    def d2(which, i):
        ref = panel.at[other, pl.ds(pl.multiple_of(i * W, W), W), half(which)]
        return remote(ref, ref, d2_s.at[0], d2_r.at[jnp.where(i < GROUPS[1][0], 0, 1)], sibling)

    def d2_arrives(group):
        ref = panel.at[other, group_rows(group), half(1 - core)]
        return remote(ref, ref, d2_s.at[0], d2_r.at[group], sibling)

    def bx(n, way):
        ref = bub.at[n, pl.ds(pl.multiple_of(x * H, H), H)]
        return remote(ref, ref, bx_s.at[way], bx_r.at[way, n], (right, left)[way])

    def bx_arrives(n, way):
        ref = bub.at[n, pl.ds(pl.multiple_of(lax.rem(x + (3, 1)[way], 4) * H, H), H)]
        return remote(ref, ref, bx_s.at[way], bx_r.at[way, n], (right, left)[way])

    def by(n, way):
        start = lax.rem(x + (3, 1)[way], 4) * H + way * (H // 2)
        ref = bub.at[n, pl.ds(pl.multiple_of(start, H // 2), H // 2)]
        return remote(ref, ref, by_s.at[way], by_r.at[way, n], (right, left)[way])

    def by_arrives(n, way):
        start = lax.rem(x + 2, 4) * H + way * (H // 2)
        ref = bub.at[n, pl.ds(pl.multiple_of(start, H // 2), H // 2)]
        return remote(ref, ref, by_s.at[way], by_r.at[way, n], (right, left)[way])

    def c(group, n):
        rows = group_rows(group)
        return remote(part_out.at[n, rows], part_in.at[n, rows], c_s.at[0], c_r.at[group, n], partner)

    def cross(group, n, step):
        first, count = GROUPS[group]
        rows = pl.ds(first * 2 * E, count * 2 * E)
        device = (lax.rem(z + step, G), row, col)
        return remote(
            cross_out.at[n, step, rows],
            cross_in.at[n, step, rows],
            z_s.at[0],
            z_r.at[group, n],
            device,
        )

    def cross_arrives(group, n):
        first, count = GROUPS[group]
        ref = cross_in.at[n, pl.ds(1, G - 1), pl.ds(first * 2 * E, count * 2 * E)]
        return remote(ref, ref, z_s.at[0], z_r.at[group, n], partner)

    def loop(count, body):
        def run(i, carry):
            body(i)
            return carry

        lax.fori_loop(0, count, run, 0)

    load_a.wait()

    def arrange(n):
        columns = pl.ds(pl.multiple_of(n * W, W), W)
        value = raw[:, columns].astype(F32)
        pieces = []
        for i in range(CHUNKS):
            for part in range(2):
                for block in range(G):
                    start = part * H + block * T + i * E
                    pieces.append(value[start : start + E])
        panel[own, :, pl.ds(pl.multiple_of(core * D + n * W, W), W)] = jnp.concatenate(pieces, axis=0).astype(BF)

    loop(CHUNKS, arrange)

    for load in (load_p, load_d, load_m):
        load.wait()
    first = jnp.broadcast_to(diag[0:1, :].astype(F32), (W, H)).T
    second = jnp.broadcast_to(diag[1:2, :].astype(F32), (W, H)).T

    def make_bubbled(n):
        columns = pl.ds(pl.multiple_of(n * W, W), W)
        real = prev[pl.ds(0, H), columns].astype(F32)
        imag = prev[pl.ds(H, H), columns].astype(F32)
        rows = pl.ds(pl.multiple_of(x * H, H), H)
        bub[n, rows, pl.ds(0, W)] = (first * real - second * imag).astype(BF)
        bub[n, rows, pl.ds(W, W)] = (first * imag + second * real).astype(BF)

    def send_bubbled(n):
        for way in (0, 1):
            bx(n, way).start()

    loop(CHUNKS, make_bubbled)
    pl.semaphore_wait(barrier, 6 + G - 1)
    loop(PIECES, lambda i: t1(i).start())

    @pl.when(yh != yl)
    def _():
        loop(PIECES, lambda i: t2(i).start())

    loop(AHEAD, send_bubbled)

    goes = []
    for step in range(G):
        target = lax.rem(z + step, G)
        index = jnp.int32(0)
        for block in range(G):
            index = jnp.where(cmap[target, row * G + block] == z, block, index)
        goes.append(index)
    comes = []
    for block in range(G):
        back = z - cmap[z, row * G + block]
        comes.append(jnp.where(back < 0, back + G, back))

    def product(group, n, slot, target):
        first, count = GROUPS[group]
        rows = group_rows(group)
        total = jnp.dot(panel[slot, rows], bub[n], preferred_element_type=F32)
        mid = W // 2
        for i in range(count):
            upper = total[i * W : i * W + mid]
            lower = total[i * W + mid : i * W + W]
            start = (first + i) * W
            target[n, pl.ds(start, mid)] = (upper[:, :W] - lower[:, W:]).astype(target.dtype)
            target[n, pl.ds(start + mid, mid)] = (upper[:, W:] + lower[:, :W]).astype(target.dtype)

    def multiply(group, n):
        product(group, n, other, part_out)
        product(group, n, yh, kept)
        c(group, n).start()

    def finish(group, n):
        first, count = GROUPS[group]
        rows = group_rows(group)
        columns = pl.ds(pl.multiple_of(core * D + n * W, W), W)
        c(group, n).wait_recv()
        value = panel[own, rows, columns].astype(F32) + (kept[n, rows] + part_in[n, rows].astype(F32))
        kept[n, rows] = value
        high = pl.ds(first * 2 * E, count * 2 * E)
        for block in range(G):
            pieces = []
            for i in range(count):
                for part in range(2):
                    start = i * W + part * (W // 2) + block * E
                    pieces.append(value[start : start + E])
            turn[block, high] = jnp.concatenate(pieces, axis=0).astype(BF)
        for step in range(G):
            if step:
                cross_out[n, step, high] = turn[goes[step], high]
                cross(group, n, step).start()
            else:
                cross_in[n, step, high] = turn[goes[step], high]

    def store(which, n):
        columns = pl.ds(pl.multiple_of(n * W, W), W)
        source = (updated, crossed)[which].at[:, columns]
        return pltpu.make_async_copy(source, (updated_out, crossed_out)[which].at[:, columns], store_sem.at[which])

    def write(n):
        columns = pl.ds(pl.multiple_of(n * W, W), W)
        value = kept[n]
        for part in range(2):
            pieces = []
            for block in range(G):
                for i in range(CHUNKS):
                    start = i * W + part * (W // 2) + block * E
                    pieces.append(value[start : start + E])
            updated[pl.ds(part * H, H), columns] = jnp.concatenate(pieces, axis=0).astype(BF)
        store(0, n).start()

    def place(n):
        columns = pl.ds(pl.multiple_of(n * W, W), W)
        for group in (0, 1):
            cross_arrives(group, n).wait_recv()
        settled[...] = cross_in[n]
        blocks = [settled[comes[block]].astype(F32) for block in range(G)]
        for part in range(2):
            pieces = []
            for block in range(G):
                for i in range(CHUNKS):
                    start = i * 2 * E + part * E
                    pieces.append(blocks[block][start : start + E])
            crossed[pl.ds(part * H, H), columns] = jnp.concatenate(pieces, axis=0).astype(BF)
        store(1, n).start()

    def relay_vertex(i):
        for piece in (2 * i, 2 * i + 1):
            t1_arrives(piece).wait_recv()

            @pl.when(yh == yl)
            def _(piece=piece):
                t2(piece).start()

    def relay_bubbled(n):
        for way in (0, 1):
            bx_arrives(n, way).wait_recv()
            by(n, way).start()

        @pl.when(n + AHEAD < CHUNKS)
        def _():
            send_bubbled(n + AHEAD)

    def share(i):
        for piece in (2 * i, 2 * i + 1):
            t2_arrives(piece).wait_recv()
        d2(core, i).start()

    def group_arrives(group):
        d1(1 - core, group).wait_recv()
        d2_arrives(group).wait_recv()

    def bubbled_arrives(n):
        for way in (0, 1):
            by_arrives(n, way).wait_recv()

    def early(n):
        bubbled_arrives(n)
        multiply(0, n)

    def gather(i):
        relay_vertex(i)

        @pl.when(i == 3)
        def _():
            d1(core, 0).start()

        @pl.when(i == 6)
        def _():
            d1(core, 1).start()
            early(2)

        @pl.when(i >= 1)
        def _():
            share(i - 1)
            relay_bubbled(i - 1)

        @pl.when(i == 4)
        def _():
            group_arrives(0)

        @pl.when((i == 4) | (i == 5))
        def _():
            early(i - 4)

    loop(CHUNKS, gather)
    share(CHUNKS - 1)

    @pl.when(yh == yl)
    def _():
        pl.semaphore_signal(go, inc=1, device_id=beside, device_id_type=MESH)

    loop(2, lambda n: finish(0, n))

    @pl.when(yh != yl)
    def _():
        pl.semaphore_wait(go, 1)

    early(3)

    def step(s):
        @pl.when(s == 0)
        def _():
            group_arrives(1)

        @pl.when(s == 1)
        def _():
            relay_bubbled(CHUNKS - 1)

        @pl.when(s < CHUNKS)
        def _():
            multiply(1, s)

        @pl.when((s >= 1) & (s < 4))
        def _():
            early(s + 3)

        @pl.when((s < 2) | ((s >= 3) & (s < 6)))
        def _():
            finish(0, jnp.where(s < 2, s + 2, s + 1))

        @pl.when((s >= 2) & (s < CHUNKS + 2))
        def _():
            finish(1, s - 2)
            write(s - 2)

        @pl.when(s >= 5)
        def _():
            place(s - 5)

    loop(CHUNKS + 5, step)

    def sent(ref, semaphore):
        remote(ref, ref, semaphore, load_sem.at[0], partner).wait_send()

    sent(panel.at[own, :, half(core)], t1_s.at[0])
    sent(panel.at[2, :, half(core)], t2_s.at[0])
    sent(panel.at[yh, :, half(core)], d1_s.at[0])
    sent(panel.at[other, :, half(core)], d2_s.at[0])
    for way in (0, 1):
        sent(bub.at[:, pl.ds(pl.multiple_of(x * H, H), H)], bx_s.at[way])
        start = lax.rem(x + (3, 1)[way], 4) * H + way * (H // 2)
        sent(bub.at[:, pl.ds(pl.multiple_of(start, H // 2), H // 2)], by_s.at[way])
    sent(part_out, c_s.at[0])
    sent(cross_out.at[:, pl.ds(1, G - 1)], z_s.at[0])
    for which in (0, 1):
        source, target = ((updated, updated_out), (crossed, crossed_out))[which]
        pltpu.make_async_copy(source, target, store_sem.at[which]).wait()


def shards(vertex, bubble, previous, cross_map):
    dma = pltpu.SemaphoreType.DMA
    updated, crossed = pl.pallas_call(
        kernel,
        out_shape=[pltpu.VMEM((D, D), BF)] * 2,
        in_specs=[
            pl.BlockSpec(memory_space=pltpu.HBM),
            pl.BlockSpec(memory_space=pltpu.HBM),
            pl.BlockSpec(memory_space=pltpu.HBM),
            pl.BlockSpec(memory_space=pltpu.HBM),
        ],
        out_specs=[pl.BlockSpec(memory_space=pl.ANY)] * 2,
        scratch_shapes=[
            pltpu.VMEM((D, D), BF),
            pltpu.VMEM((D, D), BF),
            pltpu.VMEM((3, D, 2 * D), BF),
            pltpu.VMEM((D, D), BF),
            pltpu.VMEM((D, D), BF),
            pltpu.VMEM((2, H), BF),
            pltpu.SMEM((G, G * G), jnp.int32),
            pltpu.VMEM((CHUNKS, 4 * H, 2 * W), BF),
            pltpu.VMEM((CHUNKS, D, W), F32),
            pltpu.VMEM((CHUNKS, D, W), BF),
            pltpu.VMEM((CHUNKS, D, W), BF),
            pltpu.VMEM((G, 2 * T, W), BF),
            pltpu.VMEM((G, 2 * T, W), BF),
            pltpu.VMEM((CHUNKS, G, 2 * T, W), BF),
            pltpu.VMEM((CHUNKS, G, 2 * T, W), BF),
            dma((4,)),
            dma((2,)),
            dma((1,)),
            dma((PIECES,)),
            dma((1,)),
            dma((PIECES,)),
            dma((1,)),
            dma((2,)),
            dma((1,)),
            dma((2,)),
            dma((2,)),
            dma((2, CHUNKS)),
            dma((2,)),
            dma((2, CHUNKS)),
            dma((1,)),
            dma((2, CHUNKS)),
            dma((1,)),
            dma((2, CHUNKS)),
            pltpu.SemaphoreType.REGULAR,
        ],
        compiler_params=pltpu.CompilerParams(
            collective_id=0, has_side_effects=True, vmem_limit_bytes=60 * 2**20
        ),
        cost_estimate=pl.CostEstimate(flops=8 * H * 4 * D * D, bytes_accessed=8 * D * D, transcendentals=0),
    )(vertex.reshape(D, D), bubble.reshape(2, H), previous.reshape(D, D), cross_map)
    return updated.reshape(1, 2, H, D), crossed.reshape(1, 2, H, D)


def solution(mesh):
    in_specs = (
        P("xfer", None, "row", "col"),
        P("xfer", None, "row"),
        P("xfer", None, "row", "col"),
        P(),
    )
    out_specs = (P("xfer", None, "row", "col"), P("xfer", None, "row", "col"))
    return jax.shard_map(shards, mesh=mesh, in_specs=in_specs, out_specs=out_specs, check_vma=False)
```

```python
import jax
import jax.numpy as jnp
from jax import lax
from jax.experimental import pallas as pl
from jax.experimental.pallas import tpu as pltpu
from jax.sharding import PartitionSpec as P

MESH = pl.DeviceIdType.MESH
CHUNKS = 7
W = 128
H = 448
D = 896
G = 8
T = 56
HELD = 3
AHEAD = 2
E = 8
GROUPS = ((0, 4), (4, 3))
BF = jnp.bfloat16
F32 = jnp.float32


def kernel(
    vertex,
    bubble,
    previous,
    cross_map,
    updated_out,
    crossed_out,
    updated,
    crossed,
    panel,
    mine,
    raw,
    prev,
    diag,
    cmap,
    bub,
    kept,
    part_out,
    part_in,
    turn,
    settled,
    cross_out,
    cross_in,
    load_sem,
    store_sem,
    t_s,
    t1_r,
    t2_r,
    d_s,
    d_r,
    bx_s,
    bx_r,
    by_s,
    by_r,
    c_s,
    c_r,
    z_s,
    z_r,
    go,
):
    z = lax.axis_index("xfer")
    row = lax.axis_index("row")
    col = lax.axis_index("col")
    x = lax.rem(row, 4)
    yh = lax.div(row, 4)
    yl = lax.div(col, 2)
    core = lax.rem(col, 2)
    other = 1 - yh
    right = (z, yh * 4 + lax.rem(x + 1, 4), col)
    left = (z, yh * 4 + lax.rem(x + 3, 4), col)
    beside = (z, row, (1 - yl) * 2 + core)
    across = (z, other * 4 + x, (1 - yl) * 2 + core)
    sibling = (z, row, yl * 2 + 1 - core)
    partner = (z, other * 4 + x, col)
    end = yh == yl

    def remote(src, dst, send, recv, device):
        return pltpu.make_async_remote_copy(
            src_ref=src, dst_ref=dst, send_sem=send, recv_sem=recv, device_id=device, device_id_type=MESH
        )

    load_a = pltpu.make_async_copy(vertex, raw, load_sem.at[0])
    load_p = pltpu.make_async_copy(previous, prev, load_sem.at[1])
    load_d = pltpu.make_async_copy(bubble, diag, load_sem.at[2])
    load_m = pltpu.make_async_copy(cross_map, cmap, load_sem.at[3])
    load_a.start()

    barrier = pltpu.get_barrier_semaphore()
    for device in (right, left, beside, across, sibling, partner):
        pl.semaphore_signal(barrier, inc=1, device_id=device, device_id_type=MESH)
    for step in range(1, G):
        pl.semaphore_signal(barrier, inc=1, device_id=(lax.rem(z + step, G), row, col), device_id_type=MESH)

    def half(which):
        return pl.ds(pl.multiple_of(which * D, D), D)

    def row_chunk(i):
        return pl.ds(pl.multiple_of(i * W, W), W)

    def t_end(i):
        rows = row_chunk(i)
        return remote(mine.at[rows], panel.at[yh, rows, half(core)], t_s.at[0], t1_r.at[i], beside)

    def t_middle(i):
        rows = row_chunk(i)
        return remote(mine.at[rows], panel.at[yh, rows, half(core)], t_s.at[0], t2_r.at[i], across)

    def t_far(i):
        rows = row_chunk(i)
        return remote(mine.at[rows], panel.at[yh, rows, half(core)], t_s.at[1], t2_r.at[i], partner)

    def t1_arrives(i):
        ref = panel.at[yh, row_chunk(i), half(core)]
        return remote(ref, ref, t_s.at[0], t1_r.at[i], beside)

    def t2_arrives(i):
        ref = panel.at[other, row_chunk(i), half(core)]
        return remote(ref, ref, t_s.at[0], t2_r.at[i], across)

    def group_of(i):
        return jnp.where(i < GROUPS[1][0], 0, 1)

    def group_rows(group):
        first, count = GROUPS[group]
        return pl.ds(first * W, count * W)

    def share(slot, i):
        ref = panel.at[slot, row_chunk(i), half(core)]
        return remote(ref, ref, d_s.at[0], d_r.at[jnp.where(slot == yh, 0, 1), group_of(i)], sibling)

    def share_arrives(slot, group):
        ref = panel.at[slot, group_rows(group), half(1 - core)]
        return remote(ref, ref, d_s.at[0], d_r.at[jnp.where(slot == yh, 0, 1), group], sibling)

    def bx(n, way):
        ref = bub.at[n, pl.ds(pl.multiple_of(x * H, H), H)]
        return remote(ref, ref, bx_s.at[way], bx_r.at[way, n], (right, left)[way])

    def bx_arrives(n, way):
        ref = bub.at[n, pl.ds(pl.multiple_of(lax.rem(x + (3, 1)[way], 4) * H, H), H)]
        return remote(ref, ref, bx_s.at[way], bx_r.at[way, n], (right, left)[way])

    def by(n, way):
        start = lax.rem(x + (3, 1)[way], 4) * H + way * (H // 2)
        ref = bub.at[n, pl.ds(pl.multiple_of(start, H // 2), H // 2)]
        return remote(ref, ref, by_s.at[way], by_r.at[way, n], (right, left)[way])

    def by_arrives(n, way):
        start = lax.rem(x + 2, 4) * H + way * (H // 2)
        ref = bub.at[n, pl.ds(pl.multiple_of(start, H // 2), H // 2)]
        return remote(ref, ref, by_s.at[way], by_r.at[way, n], (right, left)[way])

    def c(group, n):
        rows = group_rows(group)
        return remote(part_out.at[n, rows], part_in.at[n, rows], c_s.at[0], c_r.at[group, n], partner)

    def cross(group, n, step):
        first, count = GROUPS[group]
        rows = pl.ds(first * 2 * E, count * 2 * E)
        device = (lax.rem(z + step, G), row, col)
        return remote(
            cross_out.at[n, step, rows],
            cross_in.at[n, step, rows],
            z_s.at[0],
            z_r.at[group, n],
            device,
        )

    def cross_arrives(group, n):
        first, count = GROUPS[group]
        ref = cross_in.at[n, pl.ds(1, G - 1), pl.ds(first * 2 * E, count * 2 * E)]
        return remote(ref, ref, z_s.at[0], z_r.at[group, n], partner)

    def loop(count, body):
        def run(i, carry):
            body(i)
            return carry

        lax.fori_loop(0, count, run, 0)

    load_a.wait()
    for load in (load_p, load_d, load_m):
        load.start()

    def arrange(n):
        columns = pl.ds(pl.multiple_of(n * W, W), W)
        value = raw[:, columns].astype(F32)
        pieces = []
        for i in range(CHUNKS):
            for part in range(2):
                for block in range(G):
                    start = part * H + block * T + i * E
                    pieces.append(value[start : start + E])
        ordered = jnp.concatenate(pieces, axis=0).astype(BF)
        mine[:, columns] = ordered

        @pl.when(end)
        def _():
            panel[yh, :, pl.ds(pl.multiple_of(core * D + n * W, W), W)] = ordered

    loop(CHUNKS, arrange)
    pl.semaphore_wait(barrier, 6 + G - 1)

    @pl.when(end)
    def _():
        loop(CHUNKS, lambda i: t_end(i).start())
        loop(CHUNKS, lambda i: share(yh, i).start())

    @pl.when(jnp.logical_not(end))
    def _():
        loop(CHUNKS, lambda i: t_far(i).start())
        loop(CHUNKS, lambda i: t_middle(i).start())

    for load in (load_p, load_d, load_m):
        load.wait()
    first = jnp.broadcast_to(diag[0:1, :].astype(F32), (W, H)).T
    second = jnp.broadcast_to(diag[1:2, :].astype(F32), (W, H)).T

    def make_bubbled(n):
        columns = pl.ds(pl.multiple_of(n * W, W), W)
        real = prev[pl.ds(0, H), columns].astype(F32)
        imag = prev[pl.ds(H, H), columns].astype(F32)
        rows = pl.ds(pl.multiple_of(x * H, H), H)
        bub[n, rows, pl.ds(0, W)] = (first * real - second * imag).astype(BF)
        bub[n, rows, pl.ds(W, W)] = (first * imag + second * real).astype(BF)

    def send_bubbled(n):
        for way in (0, 1):
            bx(n, way).start()

    def first_bubbled(n):
        make_bubbled(n)
        send_bubbled(n)

    loop(AHEAD, first_bubbled)
    loop(CHUNKS - AHEAD, lambda n: make_bubbled(n + AHEAD))

    goes = []
    for step in range(G):
        target = lax.rem(z + step, G)
        index = jnp.int32(0)
        for block in range(G):
            index = jnp.where(cmap[target, row * G + block] == z, block, index)
        goes.append(index)
    comes = []
    for block in range(G):
        back = z - cmap[z, row * G + block]
        comes.append(jnp.where(back < 0, back + G, back))

    def product(group, n, slot, target):
        first, count = GROUPS[group]
        rows = group_rows(group)
        total = jnp.dot(panel[slot, rows], bub[n], preferred_element_type=F32)
        mid = W // 2
        for i in range(count):
            upper = total[i * W : i * W + mid]
            lower = total[i * W + mid : i * W + W]
            start = (first + i) * W
            target[n, pl.ds(start, mid)] = (upper[:, :W] - lower[:, W:]).astype(target.dtype)
            target[n, pl.ds(start + mid, mid)] = (upper[:, W:] + lower[:, :W]).astype(target.dtype)

    def multiply(group, n):
        product(group, n, other, part_out)
        product(group, n, yh, kept)
        if group:
            c(group, n).start()
        else:

            @pl.when(jnp.logical_not(end) | (n >= HELD))
            def _():
                c(group, n).start()


    def finish(group, n):
        first, count = GROUPS[group]
        rows = group_rows(group)
        columns = pl.ds(pl.multiple_of(n * W, W), W)
        c(group, n).wait_recv()
        value = mine[rows, columns].astype(F32) + (kept[n, rows] + part_in[n, rows].astype(F32))
        kept[n, rows] = value
        high = pl.ds(first * 2 * E, count * 2 * E)
        for block in range(G):
            pieces = []
            for i in range(count):
                for part in range(2):
                    start = i * W + part * (W // 2) + block * E
                    pieces.append(value[start : start + E])
            turn[block, high] = jnp.concatenate(pieces, axis=0).astype(BF)
        for step in range(G):
            if step:
                cross_out[n, step, high] = turn[goes[step], high]
                cross(group, n, step).start()
            else:
                cross_in[n, step, high] = turn[goes[step], high]

    def store(which, n):
        columns = pl.ds(pl.multiple_of(n * W, W), W)
        source = (updated, crossed)[which].at[:, columns]
        return pltpu.make_async_copy(source, (updated_out, crossed_out)[which].at[:, columns], store_sem.at[which])

    def write(n):
        columns = pl.ds(pl.multiple_of(n * W, W), W)
        value = kept[n]
        for part in range(2):
            pieces = []
            for block in range(G):
                for i in range(CHUNKS):
                    start = i * W + part * (W // 2) + block * E
                    pieces.append(value[start : start + E])
            updated[pl.ds(part * H, H), columns] = jnp.concatenate(pieces, axis=0).astype(BF)
        store(0, n).start()

    def place(n):
        columns = pl.ds(pl.multiple_of(n * W, W), W)
        for group in (0, 1):
            cross_arrives(group, n).wait_recv()
        settled[...] = cross_in[n]
        blocks = [settled[comes[block]].astype(F32) for block in range(G)]
        for part in range(2):
            pieces = []
            for block in range(G):
                for i in range(CHUNKS):
                    start = i * 2 * E + part * E
                    pieces.append(blocks[block][start : start + E])
            crossed[pl.ds(part * H, H), columns] = jnp.concatenate(pieces, axis=0).astype(BF)
        store(1, n).start()

    def relay_bubbled(n):
        for way in (0, 1):
            bx_arrives(n, way).wait_recv()
            by(n, way).start()

        @pl.when(n + AHEAD < CHUNKS)
        def _():
            send_bubbled(n + AHEAD)

    def group_arrives(group):
        share_arrives(yh, group).wait_recv()
        share_arrives(other, group).wait_recv()

    def bubbled_arrives(n):
        for way in (0, 1):
            by_arrives(n, way).wait_recv()

    def early(n):
        bubbled_arrives(n)
        multiply(0, n)

    def sent(ref, semaphore):
        remote(ref, ref, semaphore, load_sem.at[0], partner).wait_send()

    def pass_on(i):
        @pl.when(jnp.logical_not(end))
        def _():
            t1_arrives(i).wait_recv()
            share(yh, i).start()

        t2_arrives(i).wait_recv()
        share(other, i).start()

    def release():
        @pl.when(end)
        def _():
            pl.semaphore_wait(go, 1)
            loop(HELD, lambda n: c(0, n).start())

        @pl.when(jnp.logical_not(end))
        def _():
            sent(mine, t_s.at[0])
            pl.semaphore_signal(go, inc=1, device_id=beside, device_id_type=MESH)

    def gather(i):
        @pl.when(i == CHUNKS - 1)
        def _():
            release()

        pass_on(i)

        @pl.when((i < 2) | (i == 3) | (i == 4) | (i == 6))
        def _():
            relay_bubbled(jnp.where(i < 2, i, jnp.where(i < 5, i - 1, 4)))

        @pl.when(i == 4)
        def _():
            group_arrives(0)
            early(0)

        @pl.when(i >= 4)
        def _():
            early(i - 3)

    loop(CHUNKS, gather)
    group_arrives(1)

    def step(t):
        late = jnp.where(t == 2, 4, jnp.where(t == 5, 5, 6))

        @pl.when((t == 2) | (t == 5) | (t == 6))
        def _():
            early(late)
            multiply(1, late)

        @pl.when(t < 2)
        def _():
            loop(2, lambda n: multiply(1, 2 * t + n))

        zero = (t < 4) | (t == 8) | (t == 10) | (t == 12)

        @pl.when(zero)
        def _():
            finish(0, jnp.where(t < 4, t, t // 2))

        @pl.when(jnp.logical_not(zero) & (t < 14))
        def _():
            n = jnp.where(t < 8, t - 4, (t - 1) // 2)
            finish(1, n)
            write(n)

        @pl.when((t == 1) | (t == 3))
        def _():
            relay_bubbled(jnp.where(t == 1, 5, 6))

        @pl.when(t >= 11)
        def _():
            place(t - 11)

    loop(CHUNKS + 11, step)

    @pl.when(end)
    def _():
        sent(mine, t_s.at[0])

    @pl.when(jnp.logical_not(end))
    def _():
        sent(mine, t_s.at[1])

    sent(panel.at[:, :, half(core)], d_s.at[0])
    for way in (0, 1):
        sent(bub.at[:, pl.ds(pl.multiple_of(x * H, H), H)], bx_s.at[way])
        start = lax.rem(x + (3, 1)[way], 4) * H + way * (H // 2)
        sent(bub.at[:, pl.ds(pl.multiple_of(start, H // 2), H // 2)], by_s.at[way])
    sent(part_out, c_s.at[0])
    sent(cross_out.at[:, pl.ds(1, G - 1)], z_s.at[0])
    for which in (0, 1):
        source, target = ((updated, updated_out), (crossed, crossed_out))[which]
        pltpu.make_async_copy(source, target, store_sem.at[which]).wait()


def shards(vertex, bubble, previous, cross_map):
    dma = pltpu.SemaphoreType.DMA
    updated, crossed = pl.pallas_call(
        kernel,
        out_shape=[pltpu.VMEM((D, D), BF)] * 2,
        in_specs=[
            pl.BlockSpec(memory_space=pltpu.HBM),
            pl.BlockSpec(memory_space=pltpu.HBM),
            pl.BlockSpec(memory_space=pltpu.HBM),
            pl.BlockSpec(memory_space=pltpu.HBM),
        ],
        out_specs=[pl.BlockSpec(memory_space=pl.ANY)] * 2,
        scratch_shapes=[
            pltpu.VMEM((D, D), BF),
            pltpu.VMEM((D, D), BF),
            pltpu.VMEM((2, D, 2 * D), BF),
            pltpu.VMEM((D, D), BF),
            pltpu.VMEM((D, D), BF),
            pltpu.VMEM((D, D), BF),
            pltpu.VMEM((2, H), BF),
            pltpu.SMEM((G, G * G), jnp.int32),
            pltpu.VMEM((CHUNKS, 4 * H, 2 * W), BF),
            pltpu.VMEM((CHUNKS, D, W), F32),
            pltpu.VMEM((CHUNKS, D, W), BF),
            pltpu.VMEM((CHUNKS, D, W), BF),
            pltpu.VMEM((G, 2 * T, W), BF),
            pltpu.VMEM((G, 2 * T, W), BF),
            pltpu.VMEM((CHUNKS, G, 2 * T, W), BF),
            pltpu.VMEM((CHUNKS, G, 2 * T, W), BF),
            dma((4,)),
            dma((2,)),
            dma((2,)),
            dma((CHUNKS,)),
            dma((CHUNKS,)),
            dma((1,)),
            dma((2, 2)),
            dma((2,)),
            dma((2, CHUNKS)),
            dma((2,)),
            dma((2, CHUNKS)),
            dma((1,)),
            dma((2, CHUNKS)),
            dma((1,)),
            dma((2, CHUNKS)),
            pltpu.SemaphoreType.REGULAR,
        ],
        compiler_params=pltpu.CompilerParams(
            collective_id=0, has_side_effects=True, vmem_limit_bytes=60 * 2**20
        ),
        cost_estimate=pl.CostEstimate(flops=8 * H * 4 * D * D, bytes_accessed=8 * D * D, transcendentals=0),
    )(vertex.reshape(D, D), bubble.reshape(2, H), previous.reshape(D, D), cross_map)
    return updated.reshape(1, 2, H, D), crossed.reshape(1, 2, H, D)


def solution(mesh):
    in_specs = (
        P("xfer", None, "row", "col"),
        P("xfer", None, "row"),
        P("xfer", None, "row", "col"),
        P(),
    )
    out_specs = (P("xfer", None, "row", "col"), P("xfer", None, "row", "col"))
    return jax.shard_map(shards, mesh=mesh, in_specs=in_specs, out_specs=out_specs, check_vma=False)
```

```python
import jax
import jax.numpy as jnp
from jax import lax
from jax.experimental import pallas as pl
from jax.experimental.pallas import tpu as pltpu
from jax.sharding import PartitionSpec as P

MESH = pl.DeviceIdType.MESH
CHUNKS = 7
W = 128
H = 448
D = 896
G = 8
T = 56
HELD = 3
AHEAD = 2
E = 8
GROUPS = ((0, 2), (2, 2), (4, 3))
BF = jnp.bfloat16
F32 = jnp.float32


def kernel(
    vertex,
    bubble,
    previous,
    cross_map,
    updated_out,
    crossed_out,
    updated,
    crossed,
    panel,
    mine,
    raw,
    prev,
    diag,
    cmap,
    bub,
    kept,
    part_out,
    part_in,
    turn,
    settled,
    cross_out,
    cross_in,
    load_sem,
    store_sem,
    t_s,
    t1_r,
    t2_r,
    d_s,
    d_r,
    bx_s,
    bx_r,
    by_s,
    by_r,
    c_s,
    c_r,
    z_s,
    z_r,
    go,
):
    z = lax.axis_index("xfer")
    row = lax.axis_index("row")
    col = lax.axis_index("col")
    x = lax.rem(row, 4)
    yh = lax.div(row, 4)
    yl = lax.div(col, 2)
    core = lax.rem(col, 2)
    other = 1 - yh
    right = (z, yh * 4 + lax.rem(x + 1, 4), col)
    left = (z, yh * 4 + lax.rem(x + 3, 4), col)
    beside = (z, row, (1 - yl) * 2 + core)
    across = (z, other * 4 + x, (1 - yl) * 2 + core)
    sibling = (z, row, yl * 2 + 1 - core)
    partner = (z, other * 4 + x, col)
    end = yh == yl

    def remote(src, dst, send, recv, device):
        return pltpu.make_async_remote_copy(
            src_ref=src, dst_ref=dst, send_sem=send, recv_sem=recv, device_id=device, device_id_type=MESH
        )

    load_a = pltpu.make_async_copy(vertex, raw, load_sem.at[0])
    load_p = pltpu.make_async_copy(previous, prev, load_sem.at[1])
    load_d = pltpu.make_async_copy(bubble, diag, load_sem.at[2])
    load_m = pltpu.make_async_copy(cross_map, cmap, load_sem.at[3])
    load_a.start()

    barrier = pltpu.get_barrier_semaphore()
    for device in (right, left, beside, across, sibling, partner):
        pl.semaphore_signal(barrier, inc=1, device_id=device, device_id_type=MESH)
    for step in range(1, G):
        pl.semaphore_signal(barrier, inc=1, device_id=(lax.rem(z + step, G), row, col), device_id_type=MESH)

    def half(which):
        return pl.ds(pl.multiple_of(which * D, D), D)

    def row_chunk(i):
        return pl.ds(pl.multiple_of(i * W, W), W)

    def t_end(i):
        rows = row_chunk(i)
        return remote(mine.at[rows], panel.at[yh, rows, half(core)], t_s.at[0], t1_r.at[i], beside)

    def t_middle(i):
        rows = row_chunk(i)
        return remote(mine.at[rows], panel.at[yh, rows, half(core)], t_s.at[0], t2_r.at[i], across)

    def t_far(i):
        rows = row_chunk(i)
        return remote(mine.at[rows], panel.at[yh, rows, half(core)], t_s.at[1], t2_r.at[i], partner)

    def t1_arrives(i):
        ref = panel.at[yh, row_chunk(i), half(core)]
        return remote(ref, ref, t_s.at[0], t1_r.at[i], beside)

    def t2_arrives(i):
        ref = panel.at[other, row_chunk(i), half(core)]
        return remote(ref, ref, t_s.at[0], t2_r.at[i], across)

    def group_of(i):
        return jnp.where(i < GROUPS[1][0], 0, jnp.where(i < GROUPS[2][0], 1, 2))

    def group_rows(group):
        first, count = GROUPS[group]
        return pl.ds(first * W, count * W)

    def share(slot, i):
        ref = panel.at[slot, row_chunk(i), half(core)]
        return remote(ref, ref, d_s.at[0], d_r.at[jnp.where(slot == yh, 0, 1), group_of(i)], sibling)

    def share_arrives(slot, group):
        ref = panel.at[slot, group_rows(group), half(1 - core)]
        return remote(ref, ref, d_s.at[0], d_r.at[jnp.where(slot == yh, 0, 1), group], sibling)

    def bx(n, way):
        ref = bub.at[n, pl.ds(pl.multiple_of(x * H, H), H)]
        return remote(ref, ref, bx_s.at[way], bx_r.at[way, n], (right, left)[way])

    def bx_arrives(n, way):
        ref = bub.at[n, pl.ds(pl.multiple_of(lax.rem(x + (3, 1)[way], 4) * H, H), H)]
        return remote(ref, ref, bx_s.at[way], bx_r.at[way, n], (right, left)[way])

    def by(n, way):
        start = lax.rem(x + (3, 1)[way], 4) * H + way * (H // 2)
        ref = bub.at[n, pl.ds(pl.multiple_of(start, H // 2), H // 2)]
        return remote(ref, ref, by_s.at[way], by_r.at[way, n], (right, left)[way])

    def by_arrives(n, way):
        start = lax.rem(x + 2, 4) * H + way * (H // 2)
        ref = bub.at[n, pl.ds(pl.multiple_of(start, H // 2), H // 2)]
        return remote(ref, ref, by_s.at[way], by_r.at[way, n], (right, left)[way])

    def c(group, n):
        rows = group_rows(group)
        return remote(part_out.at[n, rows], part_in.at[n, rows], c_s.at[0], c_r.at[group, n], partner)

    def cross(group, n, step):
        first, count = GROUPS[group]
        rows = pl.ds(first * 2 * E, count * 2 * E)
        device = (lax.rem(z + step, G), row, col)
        return remote(
            cross_out.at[n, step, rows],
            cross_in.at[n, step, rows],
            z_s.at[0],
            z_r.at[group, n],
            device,
        )

    def cross_arrives(group, n):
        first, count = GROUPS[group]
        ref = cross_in.at[n, pl.ds(1, G - 1), pl.ds(first * 2 * E, count * 2 * E)]
        return remote(ref, ref, z_s.at[0], z_r.at[group, n], partner)

    def loop(count, body):
        def run(i, carry):
            body(i)
            return carry

        lax.fori_loop(0, count, run, 0)

    load_a.wait()
    for load in (load_p, load_d, load_m):
        load.start()

    def arrange(n):
        columns = pl.ds(pl.multiple_of(n * W, W), W)
        value = raw[:, columns].astype(F32)
        pieces = []
        for i in range(CHUNKS):
            for part in range(2):
                for block in range(G):
                    start = part * H + block * T + i * E
                    pieces.append(value[start : start + E])
        ordered = jnp.concatenate(pieces, axis=0).astype(BF)
        mine[:, columns] = ordered

        @pl.when(end)
        def _():
            panel[yh, :, pl.ds(pl.multiple_of(core * D + n * W, W), W)] = ordered

    loop(CHUNKS, arrange)
    pl.semaphore_wait(barrier, 6 + G - 1)

    @pl.when(end)
    def _():
        loop(CHUNKS, lambda i: t_end(i).start())
        loop(CHUNKS, lambda i: share(yh, i).start())

    @pl.when(jnp.logical_not(end))
    def _():
        loop(CHUNKS, lambda i: t_far(i).start())
        loop(CHUNKS, lambda i: t_middle(i).start())

    for load in (load_p, load_d, load_m):
        load.wait()
    first = jnp.broadcast_to(diag[0:1, :].astype(F32), (W, H)).T
    second = jnp.broadcast_to(diag[1:2, :].astype(F32), (W, H)).T

    def make_bubbled(n):
        columns = pl.ds(pl.multiple_of(n * W, W), W)
        real = prev[pl.ds(0, H), columns].astype(F32)
        imag = prev[pl.ds(H, H), columns].astype(F32)
        rows = pl.ds(pl.multiple_of(x * H, H), H)
        bub[n, rows, pl.ds(0, W)] = (first * real - second * imag).astype(BF)
        bub[n, rows, pl.ds(W, W)] = (first * imag + second * real).astype(BF)

    def send_bubbled(n):
        for way in (0, 1):
            bx(n, way).start()

    def first_bubbled(n):
        make_bubbled(n)
        send_bubbled(n)

    loop(AHEAD, first_bubbled)
    loop(CHUNKS - AHEAD, lambda n: make_bubbled(n + AHEAD))

    goes = []
    for step in range(G):
        target = lax.rem(z + step, G)
        index = jnp.int32(0)
        for block in range(G):
            index = jnp.where(cmap[target, row * G + block] == z, block, index)
        goes.append(index)
    comes = []
    for block in range(G):
        back = z - cmap[z, row * G + block]
        comes.append(jnp.where(back < 0, back + G, back))

    def product(group, n, slot, target):
        first, count = GROUPS[group]
        rows = group_rows(group)
        total = jnp.dot(panel[slot, rows], bub[n], preferred_element_type=F32)
        mid = W // 2
        for i in range(count):
            upper = total[i * W : i * W + mid]
            lower = total[i * W + mid : i * W + W]
            start = (first + i) * W
            target[n, pl.ds(start, mid)] = (upper[:, :W] - lower[:, W:]).astype(target.dtype)
            target[n, pl.ds(start + mid, mid)] = (upper[:, W:] + lower[:, :W]).astype(target.dtype)

    def multiply(group, n):
        product(group, n, other, part_out)
        product(group, n, yh, kept)
        if group == 2:
            c(group, n).start()
        else:

            @pl.when(jnp.logical_not(end) | (n >= HELD))
            def _():
                c(group, n).start()


    def finish(group, n):
        first, count = GROUPS[group]
        rows = group_rows(group)
        columns = pl.ds(pl.multiple_of(n * W, W), W)
        c(group, n).wait_recv()
        value = mine[rows, columns].astype(F32) + (kept[n, rows] + part_in[n, rows].astype(F32))
        kept[n, rows] = value
        high = pl.ds(first * 2 * E, count * 2 * E)
        for block in range(G):
            pieces = []
            for i in range(count):
                for part in range(2):
                    start = i * W + part * (W // 2) + block * E
                    pieces.append(value[start : start + E])
            turn[block, high] = jnp.concatenate(pieces, axis=0).astype(BF)
        for step in range(G):
            if step:
                cross_out[n, step, high] = turn[goes[step], high]
                cross(group, n, step).start()
            else:
                cross_in[n, step, high] = turn[goes[step], high]

    def store(which, n):
        columns = pl.ds(pl.multiple_of(n * W, W), W)
        source = (updated, crossed)[which].at[:, columns]
        return pltpu.make_async_copy(source, (updated_out, crossed_out)[which].at[:, columns], store_sem.at[which])

    def write(n):
        columns = pl.ds(pl.multiple_of(n * W, W), W)
        value = kept[n]
        for part in range(2):
            pieces = []
            for block in range(G):
                for i in range(CHUNKS):
                    start = i * W + part * (W // 2) + block * E
                    pieces.append(value[start : start + E])
            updated[pl.ds(part * H, H), columns] = jnp.concatenate(pieces, axis=0).astype(BF)
        store(0, n).start()

    def place(n):
        columns = pl.ds(pl.multiple_of(n * W, W), W)
        for group in (0, 1, 2):
            cross_arrives(group, n).wait_recv()
        settled[...] = cross_in[n]
        blocks = [settled[comes[block]].astype(F32) for block in range(G)]
        for part in range(2):
            pieces = []
            for block in range(G):
                for i in range(CHUNKS):
                    start = i * 2 * E + part * E
                    pieces.append(blocks[block][start : start + E])
            crossed[pl.ds(part * H, H), columns] = jnp.concatenate(pieces, axis=0).astype(BF)
        store(1, n).start()

    def relay_bubbled(n):
        for way in (0, 1):
            bx_arrives(n, way).wait_recv()
            by(n, way).start()

        @pl.when(n + AHEAD < CHUNKS)
        def _():
            send_bubbled(n + AHEAD)

    def group_arrives(group):
        share_arrives(yh, group).wait_recv()
        share_arrives(other, group).wait_recv()

    def bubbled_arrives(n):
        for way in (0, 1):
            by_arrives(n, way).wait_recv()

    def early(n):
        bubbled_arrives(n)
        multiply(0, n)
        multiply(1, n)

    def sent(ref, semaphore):
        remote(ref, ref, semaphore, load_sem.at[0], partner).wait_send()

    def pass_on(i):
        @pl.when(jnp.logical_not(end))
        def _():
            t1_arrives(i).wait_recv()
            share(yh, i).start()

        t2_arrives(i).wait_recv()
        share(other, i).start()

    def release():
        @pl.when(end)
        def _():
            pl.semaphore_wait(go, 1)

            def start(n):
                c(0, n).start()
                c(1, n).start()

            loop(HELD, start)

        @pl.when(jnp.logical_not(end))
        def _():
            sent(mine, t_s.at[0])
            pl.semaphore_signal(go, inc=1, device_id=beside, device_id_type=MESH)

    def gather(i):
        @pl.when(i == CHUNKS - 1)
        def _():
            release()

        pass_on(i)

        @pl.when((i < 2) | (i == 3) | (i == 4) | (i == 6))
        def _():
            relay_bubbled(jnp.where(i < 2, i, jnp.where(i < 5, i - 1, 4)))

        @pl.when(i == CHUNKS - 1)
        def _():
            finish(0, 0)

        @pl.when(i == 4)
        def _():
            group_arrives(0)
            group_arrives(1)
            early(0)

        @pl.when(i >= 4)
        def _():
            early(i - 3)

    loop(CHUNKS, gather)
    finish(1, 0)
    group_arrives(2)

    def step(t):
        late = jnp.where(t == 2, 4, jnp.where(t == 5, 5, 6))
        zero = (t < 3) | (t == 7) | (t == 9) | (t == 11)

        @pl.when((t == 5) | (t == 6))
        def _():
            early(late)
            multiply(2, late)

        @pl.when(t < 3)
        def _():
            multiply(2, t)

        @pl.when((t == 1) | (t == 3))
        def _():
            relay_bubbled(jnp.where(t == 1, 5, 6))

        @pl.when(zero)
        def _():
            n = jnp.where(t < 3, t + 1, (t + 1) // 2)
            finish(0, n)
            finish(1, n)

        @pl.when(t == 2)
        def _():
            multiply(2, 3)
            early(4)
            multiply(2, 4)

        @pl.when(jnp.logical_not(zero) & (t < 13))
        def _():
            n = jnp.where(t < 7, t - 3, t // 2)
            finish(2, n)
            write(n)

        @pl.when(t >= 10)
        def _():
            place(t - 10)

    loop(CHUNKS + 10, step)

    @pl.when(end)
    def _():
        sent(mine, t_s.at[0])

    @pl.when(jnp.logical_not(end))
    def _():
        sent(mine, t_s.at[1])

    sent(panel.at[:, :, half(core)], d_s.at[0])
    for way in (0, 1):
        sent(bub.at[:, pl.ds(pl.multiple_of(x * H, H), H)], bx_s.at[way])
        start = lax.rem(x + (3, 1)[way], 4) * H + way * (H // 2)
        sent(bub.at[:, pl.ds(pl.multiple_of(start, H // 2), H // 2)], by_s.at[way])
    sent(part_out, c_s.at[0])
    sent(cross_out.at[:, pl.ds(1, G - 1)], z_s.at[0])
    for which in (0, 1):
        source, target = ((updated, updated_out), (crossed, crossed_out))[which]
        pltpu.make_async_copy(source, target, store_sem.at[which]).wait()


def shards(vertex, bubble, previous, cross_map):
    dma = pltpu.SemaphoreType.DMA
    updated, crossed = pl.pallas_call(
        kernel,
        out_shape=[pltpu.VMEM((D, D), BF)] * 2,
        in_specs=[
            pl.BlockSpec(memory_space=pltpu.HBM),
            pl.BlockSpec(memory_space=pltpu.HBM),
            pl.BlockSpec(memory_space=pltpu.HBM),
            pl.BlockSpec(memory_space=pltpu.HBM),
        ],
        out_specs=[pl.BlockSpec(memory_space=pl.ANY)] * 2,
        scratch_shapes=[
            pltpu.VMEM((D, D), BF),
            pltpu.VMEM((D, D), BF),
            pltpu.VMEM((2, D, 2 * D), BF),
            pltpu.VMEM((D, D), BF),
            pltpu.VMEM((D, D), BF),
            pltpu.VMEM((D, D), BF),
            pltpu.VMEM((2, H), BF),
            pltpu.SMEM((G, G * G), jnp.int32),
            pltpu.VMEM((CHUNKS, 4 * H, 2 * W), BF),
            pltpu.VMEM((CHUNKS, D, W), F32),
            pltpu.VMEM((CHUNKS, D, W), BF),
            pltpu.VMEM((CHUNKS, D, W), BF),
            pltpu.VMEM((G, 2 * T, W), BF),
            pltpu.VMEM((G, 2 * T, W), BF),
            pltpu.VMEM((CHUNKS, G, 2 * T, W), BF),
            pltpu.VMEM((CHUNKS, G, 2 * T, W), BF),
            dma((4,)),
            dma((2,)),
            dma((2,)),
            dma((CHUNKS,)),
            dma((CHUNKS,)),
            dma((1,)),
            dma((2, 3)),
            dma((2,)),
            dma((2, CHUNKS)),
            dma((2,)),
            dma((2, CHUNKS)),
            dma((1,)),
            dma((3, CHUNKS)),
            dma((1,)),
            dma((3, CHUNKS)),
            pltpu.SemaphoreType.REGULAR,
        ],
        compiler_params=pltpu.CompilerParams(
            collective_id=0, has_side_effects=True, vmem_limit_bytes=60 * 2**20
        ),
        cost_estimate=pl.CostEstimate(flops=8 * H * 4 * D * D, bytes_accessed=8 * D * D, transcendentals=0),
    )(vertex.reshape(D, D), bubble.reshape(2, H), previous.reshape(D, D), cross_map)
    return updated.reshape(1, 2, H, D), crossed.reshape(1, 2, H, D)


def solution(mesh):
    in_specs = (
        P("xfer", None, "row", "col"),
        P("xfer", None, "row"),
        P("xfer", None, "row", "col"),
        P(),
    )
    out_specs = (P("xfer", None, "row", "col"), P("xfer", None, "row", "col"))
    return jax.shard_map(shards, mesh=mesh, in_specs=in_specs, out_specs=out_specs, check_vma=False)
```

```python
import jax
import jax.numpy as jnp
from jax import lax
from jax.experimental import pallas as pl
from jax.experimental.pallas import tpu as pltpu
from jax.sharding import PartitionSpec as P

MESH = pl.DeviceIdType.MESH
CHUNKS = 7
W = 128
H = 448
D = 896
G = 8
T = 56
HELD = 3
FAR_FIRST = (4, 3, 5, 2, 6, 1, 7, 0)
AHEAD = 2
E = 8
GROUPS = ((0, 2), (2, 2), (4, 3))
BF = jnp.bfloat16
F32 = jnp.float32


def kernel(
    vertex,
    bubble,
    previous,
    cross_map,
    updated_out,
    crossed_out,
    updated,
    crossed,
    panel,
    mine,
    raw,
    prev,
    diag,
    cmap,
    bub,
    kept,
    part_out,
    part_in,
    turn,
    settled,
    cross_out,
    cross_in,
    load_sem,
    store_sem,
    t_s,
    t1_r,
    t2_r,
    d_s,
    d_r,
    bx_s,
    bx_r,
    by_s,
    by_r,
    c_s,
    c_r,
    z_s,
    z_r,
    go,
):
    z = lax.axis_index("xfer")
    row = lax.axis_index("row")
    col = lax.axis_index("col")
    x = lax.rem(row, 4)
    yh = lax.div(row, 4)
    yl = lax.div(col, 2)
    core = lax.rem(col, 2)
    other = 1 - yh
    right = (z, yh * 4 + lax.rem(x + 1, 4), col)
    left = (z, yh * 4 + lax.rem(x + 3, 4), col)
    beside = (z, row, (1 - yl) * 2 + core)
    across = (z, other * 4 + x, (1 - yl) * 2 + core)
    sibling = (z, row, yl * 2 + 1 - core)
    partner = (z, other * 4 + x, col)
    end = yh == yl

    def remote(src, dst, send, recv, device):
        return pltpu.make_async_remote_copy(
            src_ref=src, dst_ref=dst, send_sem=send, recv_sem=recv, device_id=device, device_id_type=MESH
        )

    load_a = pltpu.make_async_copy(vertex, raw, load_sem.at[0])
    load_p = pltpu.make_async_copy(previous, prev, load_sem.at[1])
    load_d = pltpu.make_async_copy(bubble, diag, load_sem.at[2])
    load_m = pltpu.make_async_copy(cross_map, cmap, load_sem.at[3])
    load_a.start()

    barrier = pltpu.get_barrier_semaphore()
    for device in (right, left, beside, across, sibling, partner):
        pl.semaphore_signal(barrier, inc=1, device_id=device, device_id_type=MESH)
    for step in range(1, G):
        pl.semaphore_signal(barrier, inc=1, device_id=(lax.rem(z + step, G), row, col), device_id_type=MESH)

    def half(which):
        return pl.ds(pl.multiple_of(which * D, D), D)

    def row_chunk(i):
        return pl.ds(pl.multiple_of(i * W, W), W)

    def t_end(i):
        rows = row_chunk(i)
        return remote(mine.at[rows], panel.at[yh, rows, half(core)], t_s.at[0], t1_r.at[i], beside)

    def t_middle(i):
        rows = row_chunk(i)
        return remote(mine.at[rows], panel.at[yh, rows, half(core)], t_s.at[0], t2_r.at[i], across)

    def t_far(i):
        rows = row_chunk(i)
        return remote(mine.at[rows], panel.at[yh, rows, half(core)], t_s.at[1], t2_r.at[i], partner)

    def t1_arrives(i):
        ref = panel.at[yh, row_chunk(i), half(core)]
        return remote(ref, ref, t_s.at[0], t1_r.at[i], beside)

    def t2_arrives(i):
        ref = panel.at[other, row_chunk(i), half(core)]
        return remote(ref, ref, t_s.at[0], t2_r.at[i], across)

    def group_of(i):
        return jnp.where(i < GROUPS[1][0], 0, jnp.where(i < GROUPS[2][0], 1, 2))

    def group_rows(group):
        first, count = GROUPS[group]
        return pl.ds(first * W, count * W)

    def share(slot, i):
        ref = panel.at[slot, row_chunk(i), half(core)]
        return remote(ref, ref, d_s.at[0], d_r.at[jnp.where(slot == yh, 0, 1), group_of(i)], sibling)

    def share_arrives(slot, group):
        ref = panel.at[slot, group_rows(group), half(1 - core)]
        return remote(ref, ref, d_s.at[0], d_r.at[jnp.where(slot == yh, 0, 1), group], sibling)

    def bx(n, way):
        ref = bub.at[n, pl.ds(pl.multiple_of(x * H, H), H)]
        return remote(ref, ref, bx_s.at[way], bx_r.at[way, n], (right, left)[way])

    def bx_arrives(n, way):
        ref = bub.at[n, pl.ds(pl.multiple_of(lax.rem(x + (3, 1)[way], 4) * H, H), H)]
        return remote(ref, ref, bx_s.at[way], bx_r.at[way, n], (right, left)[way])

    def by(n, way):
        start = lax.rem(x + (3, 1)[way], 4) * H + way * (H // 2)
        ref = bub.at[n, pl.ds(pl.multiple_of(start, H // 2), H // 2)]
        return remote(ref, ref, by_s.at[way], by_r.at[way, n], (right, left)[way])

    def by_arrives(n, way):
        start = lax.rem(x + 2, 4) * H + way * (H // 2)
        ref = bub.at[n, pl.ds(pl.multiple_of(start, H // 2), H // 2)]
        return remote(ref, ref, by_s.at[way], by_r.at[way, n], (right, left)[way])

    def c(group, n):
        rows = group_rows(group)
        return remote(part_out.at[n, rows], part_in.at[n, rows], c_s.at[0], c_r.at[group, n], partner)

    def cross(group, n, step):
        first, count = GROUPS[group]
        rows = pl.ds(first * 2 * E, count * 2 * E)
        device = (lax.rem(z + step, G), row, col)
        return remote(
            cross_out.at[n, step, rows],
            cross_in.at[n, step, rows],
            z_s.at[0],
            z_r.at[group, n],
            device,
        )

    def cross_arrives(group, n):
        first, count = GROUPS[group]
        ref = cross_in.at[n, pl.ds(1, G - 1), pl.ds(first * 2 * E, count * 2 * E)]
        return remote(ref, ref, z_s.at[0], z_r.at[group, n], partner)

    def loop(count, body):
        def run(i, carry):
            body(i)
            return carry

        lax.fori_loop(0, count, run, 0)

    load_a.wait()
    for load in (load_p, load_d, load_m):
        load.start()

    def arrange(n):
        columns = pl.ds(pl.multiple_of(n * W, W), W)
        value = raw[:, columns].astype(F32)
        pieces = []
        for i in range(CHUNKS):
            for part in range(2):
                for block in range(G):
                    start = part * H + block * T + i * E
                    pieces.append(value[start : start + E])
        ordered = jnp.concatenate(pieces, axis=0).astype(BF)
        mine[:, columns] = ordered

        @pl.when(end)
        def _():
            panel[yh, :, pl.ds(pl.multiple_of(core * D + n * W, W), W)] = ordered

    loop(CHUNKS, arrange)
    pl.semaphore_wait(barrier, 6 + G - 1)

    @pl.when(end)
    def _():
        loop(CHUNKS, lambda i: t_end(i).start())
        loop(CHUNKS, lambda i: share(yh, i).start())

    @pl.when(jnp.logical_not(end))
    def _():
        loop(CHUNKS, lambda i: t_far(i).start())
        loop(CHUNKS, lambda i: t_middle(i).start())

    for load in (load_p, load_d, load_m):
        load.wait()
    first = jnp.broadcast_to(diag[0:1, :].astype(F32), (W, H)).T
    second = jnp.broadcast_to(diag[1:2, :].astype(F32), (W, H)).T

    def make_bubbled(n):
        columns = pl.ds(pl.multiple_of(n * W, W), W)
        real = prev[pl.ds(0, H), columns].astype(F32)
        imag = prev[pl.ds(H, H), columns].astype(F32)
        rows = pl.ds(pl.multiple_of(x * H, H), H)
        bub[n, rows, pl.ds(0, W)] = (first * real - second * imag).astype(BF)
        bub[n, rows, pl.ds(W, W)] = (first * imag + second * real).astype(BF)

    def send_bubbled(n):
        for way in (0, 1):
            bx(n, way).start()

    def first_bubbled(n):
        make_bubbled(n)
        send_bubbled(n)

    loop(AHEAD, first_bubbled)
    loop(CHUNKS - AHEAD, lambda n: make_bubbled(n + AHEAD))

    goes = []
    for step in range(G):
        target = lax.rem(z + step, G)
        index = jnp.int32(0)
        for block in range(G):
            index = jnp.where(cmap[target, row * G + block] == z, block, index)
        goes.append(index)
    comes = []
    for block in range(G):
        back = z - cmap[z, row * G + block]
        comes.append(jnp.where(back < 0, back + G, back))

    def product(group, n, slot, target):
        first, count = GROUPS[group]
        rows = group_rows(group)
        total = jnp.dot(panel[slot, rows], bub[n], preferred_element_type=F32)
        mid = W // 2
        for i in range(count):
            upper = total[i * W : i * W + mid]
            lower = total[i * W + mid : i * W + W]
            start = (first + i) * W
            target[n, pl.ds(start, mid)] = (upper[:, :W] - lower[:, W:]).astype(target.dtype)
            target[n, pl.ds(start + mid, mid)] = (upper[:, W:] + lower[:, :W]).astype(target.dtype)

    def multiply(group, n):
        product(group, n, other, part_out)
        product(group, n, yh, kept)
        if group == 2:
            c(group, n).start()
        else:

            @pl.when(jnp.logical_not(end) | (n >= HELD))
            def _():
                c(group, n).start()


    def finish(group, n):
        first, count = GROUPS[group]
        rows = group_rows(group)
        columns = pl.ds(pl.multiple_of(n * W, W), W)
        c(group, n).wait_recv()
        value = mine[rows, columns].astype(F32) + (kept[n, rows] + part_in[n, rows].astype(F32))
        kept[n, rows] = value
        high = pl.ds(first * 2 * E, count * 2 * E)
        for block in range(G):
            pieces = []
            for i in range(count):
                for part in range(2):
                    start = i * W + part * (W // 2) + block * E
                    pieces.append(value[start : start + E])
            turn[block, high] = jnp.concatenate(pieces, axis=0).astype(BF)
        for step in FAR_FIRST:
            if step:
                cross_out[n, step, high] = turn[goes[step], high]
                cross(group, n, step).start()
            else:
                cross_in[n, step, high] = turn[goes[step], high]

    def store(which, n):
        columns = pl.ds(pl.multiple_of(n * W, W), W)
        source = (updated, crossed)[which].at[:, columns]
        return pltpu.make_async_copy(source, (updated_out, crossed_out)[which].at[:, columns], store_sem.at[which])

    def write(n):
        columns = pl.ds(pl.multiple_of(n * W, W), W)
        value = kept[n]
        for part in range(2):
            pieces = []
            for block in range(G):
                for i in range(CHUNKS):
                    start = i * W + part * (W // 2) + block * E
                    pieces.append(value[start : start + E])
            updated[pl.ds(part * H, H), columns] = jnp.concatenate(pieces, axis=0).astype(BF)
        store(0, n).start()

    def place(n):
        columns = pl.ds(pl.multiple_of(n * W, W), W)
        for group in (0, 1, 2):
            cross_arrives(group, n).wait_recv()
        settled[...] = cross_in[n]
        blocks = [settled[comes[block]].astype(F32) for block in range(G)]
        for part in range(2):
            pieces = []
            for block in range(G):
                for i in range(CHUNKS):
                    start = i * 2 * E + part * E
                    pieces.append(blocks[block][start : start + E])
            crossed[pl.ds(part * H, H), columns] = jnp.concatenate(pieces, axis=0).astype(BF)
        store(1, n).start()

    def relay_bubbled(n):
        for way in (0, 1):
            bx_arrives(n, way).wait_recv()
            by(n, way).start()

        @pl.when(n + AHEAD < CHUNKS)
        def _():
            send_bubbled(n + AHEAD)

    def group_arrives(group):
        share_arrives(yh, group).wait_recv()
        share_arrives(other, group).wait_recv()

    def bubbled_arrives(n):
        for way in (0, 1):
            by_arrives(n, way).wait_recv()

    def early(n):
        bubbled_arrives(n)
        multiply(0, n)
        multiply(1, n)

    def sent(ref, semaphore):
        remote(ref, ref, semaphore, load_sem.at[0], partner).wait_send()

    def pass_on(i):
        @pl.when(jnp.logical_not(end))
        def _():
            t1_arrives(i).wait_recv()
            share(yh, i).start()

        t2_arrives(i).wait_recv()
        share(other, i).start()

    def release():
        @pl.when(end)
        def _():
            pl.semaphore_wait(go, 1)

            def start(n):
                c(0, n).start()
                c(1, n).start()

            loop(HELD, start)

        @pl.when(jnp.logical_not(end))
        def _():
            sent(mine, t_s.at[0])
            pl.semaphore_signal(go, inc=1, device_id=beside, device_id_type=MESH)

    def gather(i):
        @pl.when(i == CHUNKS - 1)
        def _():
            release()

        pass_on(i)

        @pl.when((i < 2) | (i == 3) | (i == 4) | (i == 6))
        def _():
            relay_bubbled(jnp.where(i < 2, i, jnp.where(i < 5, i - 1, 4)))

        @pl.when(i == CHUNKS - 1)
        def _():
            finish(0, 0)

        @pl.when(i == 4)
        def _():
            group_arrives(0)
            group_arrives(1)
            early(0)

        @pl.when(i >= 4)
        def _():
            early(i - 3)

    loop(CHUNKS, gather)
    finish(1, 0)
    group_arrives(2)

    def step(t):
        late = jnp.where(t == 2, 4, jnp.where(t == 5, 5, 6))
        zero = (t < 3) | (t == 7) | (t == 9) | (t == 11)

        @pl.when((t == 5) | (t == 6))
        def _():
            early(late)
            multiply(2, late)

        @pl.when(t < 3)
        def _():
            multiply(2, t)

        @pl.when((t == 1) | (t == 3))
        def _():
            relay_bubbled(jnp.where(t == 1, 5, 6))

        @pl.when(zero)
        def _():
            n = jnp.where(t < 3, t + 1, (t + 1) // 2)
            finish(0, n)
            finish(1, n)

        @pl.when(t == 2)
        def _():
            multiply(2, 3)
            early(4)
            multiply(2, 4)

        @pl.when(jnp.logical_not(zero) & (t < 13))
        def _():
            n = jnp.where(t < 7, t - 3, t // 2)
            finish(2, n)
            write(n)

        @pl.when(t >= 10)
        def _():
            place(t - 10)

    loop(CHUNKS + 10, step)

    @pl.when(end)
    def _():
        sent(mine, t_s.at[0])

    @pl.when(jnp.logical_not(end))
    def _():
        sent(mine, t_s.at[1])

    sent(panel.at[:, :, half(core)], d_s.at[0])
    for way in (0, 1):
        sent(bub.at[:, pl.ds(pl.multiple_of(x * H, H), H)], bx_s.at[way])
        start = lax.rem(x + (3, 1)[way], 4) * H + way * (H // 2)
        sent(bub.at[:, pl.ds(pl.multiple_of(start, H // 2), H // 2)], by_s.at[way])
    sent(part_out, c_s.at[0])
    sent(cross_out.at[:, pl.ds(1, G - 1)], z_s.at[0])
    for which in (0, 1):
        source, target = ((updated, updated_out), (crossed, crossed_out))[which]
        pltpu.make_async_copy(source, target, store_sem.at[which]).wait()


def hand_over(updated, crossed, updated_out, crossed_out, sem):
    copies = [
        pltpu.make_async_copy(updated, updated_out, sem.at[0]),
        pltpu.make_async_copy(crossed, crossed_out, sem.at[1]),
    ]
    for copy in copies:
        copy.start()
    for copy in copies:
        copy.wait()


def shards(vertex, bubble, previous, cross_map):
    dma = pltpu.SemaphoreType.DMA
    updated, crossed = pl.pallas_call(
        kernel,
        out_shape=[pltpu.VMEM((D, D), BF)] * 2,
        in_specs=[
            pl.BlockSpec(memory_space=pltpu.HBM),
            pl.BlockSpec(memory_space=pltpu.HBM),
            pl.BlockSpec(memory_space=pltpu.HBM),
            pl.BlockSpec(memory_space=pltpu.HBM),
        ],
        out_specs=[pl.BlockSpec(memory_space=pl.ANY)] * 2,
        scratch_shapes=[
            pltpu.VMEM((D, D), BF),
            pltpu.VMEM((D, D), BF),
            pltpu.VMEM((2, D, 2 * D), BF),
            pltpu.VMEM((D, D), BF),
            pltpu.VMEM((D, D), BF),
            pltpu.VMEM((D, D), BF),
            pltpu.VMEM((2, H), BF),
            pltpu.SMEM((G, G * G), jnp.int32),
            pltpu.VMEM((CHUNKS, 4 * H, 2 * W), BF),
            pltpu.VMEM((CHUNKS, D, W), F32),
            pltpu.VMEM((CHUNKS, D, W), BF),
            pltpu.VMEM((CHUNKS, D, W), BF),
            pltpu.VMEM((G, 2 * T, W), BF),
            pltpu.VMEM((G, 2 * T, W), BF),
            pltpu.VMEM((CHUNKS, G, 2 * T, W), BF),
            pltpu.VMEM((CHUNKS, G, 2 * T, W), BF),
            dma((4,)),
            dma((2,)),
            dma((2,)),
            dma((CHUNKS,)),
            dma((CHUNKS,)),
            dma((1,)),
            dma((2, 3)),
            dma((2,)),
            dma((2, CHUNKS)),
            dma((2,)),
            dma((2, CHUNKS)),
            dma((1,)),
            dma((3, CHUNKS)),
            dma((1,)),
            dma((3, CHUNKS)),
            pltpu.SemaphoreType.REGULAR,
        ],
        compiler_params=pltpu.CompilerParams(
            collective_id=0, has_side_effects=True, vmem_limit_bytes=60 * 2**20
        ),
        cost_estimate=pl.CostEstimate(flops=8 * H * 4 * D * D, bytes_accessed=8 * D * D, transcendentals=0),
    )(vertex.reshape(D, D), bubble.reshape(2, H), previous.reshape(D, D), cross_map)
    updated, crossed = pl.pallas_call(
        hand_over,
        out_shape=[jax.ShapeDtypeStruct((D, D), BF)] * 2,
        in_specs=[pl.BlockSpec(memory_space=pl.ANY)] * 2,
        out_specs=[pl.BlockSpec(memory_space=pl.ANY)] * 2,
        scratch_shapes=[pltpu.SemaphoreType.DMA((2,))],
        compiler_params=pltpu.CompilerParams(vmem_limit_bytes=4 * 2**20),
        cost_estimate=pl.CostEstimate(flops=0, bytes_accessed=8 * D * D, transcendentals=0),
    )(updated, crossed)
    return updated.reshape(1, 2, H, D), crossed.reshape(1, 2, H, D)


def solution(mesh):
    in_specs = (
        P("xfer", None, "row", "col"),
        P("xfer", None, "row"),
        P("xfer", None, "row", "col"),
        P(),
    )
    out_specs = (P("xfer", None, "row", "col"), P("xfer", None, "row", "col"))
    return jax.shard_map(shards, mesh=mesh, in_specs=in_specs, out_specs=out_specs, check_vma=False)
```

```python
import jax
import jax.numpy as jnp
from jax import lax
from jax.experimental import pallas as pl
from jax.experimental.pallas import tpu as pltpu
from jax.sharding import PartitionSpec as P

MESH = pl.DeviceIdType.MESH
CHUNKS = 7
W = 128
H = 448
D = 896
G = 8
T = 56
HELD = 3
FAR_FIRST = (4, 3, 5, 2, 6, 1, 7, 0)
AHEAD = 2
E = 8
GROUPS = ((0, 2), (2, 2), (4, 3))
BF = jnp.bfloat16
F32 = jnp.float32


def kernel(
    vertex,
    bubble,
    previous,
    cross_map,
    updated_out,
    crossed_out,
    updated,
    crossed,
    panel,
    mine,
    raw,
    prev,
    cmap,
    bub,
    kept,
    part_out,
    part_in,
    turn,
    settled,
    cross_out,
    cross_in,
    load_sem,
    store_sem,
    t_s,
    t1_r,
    t2_r,
    d_s,
    d_r,
    bx_s,
    bx_r,
    by_s,
    by_r,
    c_s,
    c_r,
    z_s,
    z_r,
    go,
):
    z = lax.axis_index("xfer")
    row = lax.axis_index("row")
    col = lax.axis_index("col")
    x = lax.rem(row, 4)
    yh = lax.div(row, 4)
    yl = lax.div(col, 2)
    core = lax.rem(col, 2)
    other = 1 - yh
    right = (z, yh * 4 + lax.rem(x + 1, 4), col)
    left = (z, yh * 4 + lax.rem(x + 3, 4), col)
    beside = (z, row, (1 - yl) * 2 + core)
    across = (z, other * 4 + x, (1 - yl) * 2 + core)
    sibling = (z, row, yl * 2 + 1 - core)
    partner = (z, other * 4 + x, col)
    end = yh == yl

    def remote(src, dst, send, recv, device):
        return pltpu.make_async_remote_copy(
            src_ref=src, dst_ref=dst, send_sem=send, recv_sem=recv, device_id=device, device_id_type=MESH
        )

    load_a = pltpu.make_async_copy(vertex, raw, load_sem.at[0])
    load_p = pltpu.make_async_copy(previous, prev, load_sem.at[1])
    load_m = pltpu.make_async_copy(cross_map, cmap, load_sem.at[2])
    load_a.start()

    barrier = pltpu.get_barrier_semaphore()
    for device in (right, left, beside, across, sibling, partner):
        pl.semaphore_signal(barrier, inc=1, device_id=device, device_id_type=MESH)
    for step in range(1, G):
        pl.semaphore_signal(barrier, inc=1, device_id=(lax.rem(z + step, G), row, col), device_id_type=MESH)

    def half(which):
        return pl.ds(pl.multiple_of(which * D, D), D)

    def row_chunk(i):
        return pl.ds(pl.multiple_of(i * W, W), W)

    def t_end(i):
        rows = row_chunk(i)
        return remote(mine.at[rows], panel.at[yh, rows, half(core)], t_s.at[0], t1_r.at[i], beside)

    def t_middle(i):
        rows = row_chunk(i)
        return remote(mine.at[rows], panel.at[yh, rows, half(core)], t_s.at[0], t2_r.at[i], across)

    def t_far(i):
        rows = row_chunk(i)
        return remote(mine.at[rows], panel.at[yh, rows, half(core)], t_s.at[1], t2_r.at[i], partner)

    def t1_arrives(i):
        ref = panel.at[yh, row_chunk(i), half(core)]
        return remote(ref, ref, t_s.at[0], t1_r.at[i], beside)

    def t2_arrives(i):
        ref = panel.at[other, row_chunk(i), half(core)]
        return remote(ref, ref, t_s.at[0], t2_r.at[i], across)

    def group_of(i):
        return jnp.where(i < GROUPS[1][0], 0, jnp.where(i < GROUPS[2][0], 1, 2))

    def group_rows(group):
        first, count = GROUPS[group]
        return pl.ds(first * W, count * W)

    def share(slot, i):
        ref = panel.at[slot, row_chunk(i), half(core)]
        return remote(ref, ref, d_s.at[0], d_r.at[jnp.where(slot == yh, 0, 1), group_of(i)], sibling)

    def share_arrives(slot, group):
        ref = panel.at[slot, group_rows(group), half(1 - core)]
        return remote(ref, ref, d_s.at[0], d_r.at[jnp.where(slot == yh, 0, 1), group], sibling)

    def bx(n, way):
        ref = bub.at[n, pl.ds(pl.multiple_of(x * H, H), H)]
        return remote(ref, ref, bx_s.at[way], bx_r.at[way, n], (right, left)[way])

    def bx_arrives(n, way):
        ref = bub.at[n, pl.ds(pl.multiple_of(lax.rem(x + (3, 1)[way], 4) * H, H), H)]
        return remote(ref, ref, bx_s.at[way], bx_r.at[way, n], (right, left)[way])

    def by(n, way):
        start = lax.rem(x + (3, 1)[way], 4) * H + way * (H // 2)
        ref = bub.at[n, pl.ds(pl.multiple_of(start, H // 2), H // 2)]
        return remote(ref, ref, by_s.at[way], by_r.at[way, n], (right, left)[way])

    def by_arrives(n, way):
        start = lax.rem(x + 2, 4) * H + way * (H // 2)
        ref = bub.at[n, pl.ds(pl.multiple_of(start, H // 2), H // 2)]
        return remote(ref, ref, by_s.at[way], by_r.at[way, n], (right, left)[way])

    def c(group, n):
        rows = group_rows(group)
        return remote(part_out.at[n, rows], part_in.at[n, rows], c_s.at[0], c_r.at[group, n], partner)

    def cross(group, n, step):
        first, count = GROUPS[group]
        rows = pl.ds(first * 2 * E, count * 2 * E)
        device = (lax.rem(z + step, G), row, col)
        return remote(
            cross_out.at[n, step, rows],
            cross_in.at[n, step, rows],
            z_s.at[0],
            z_r.at[group, n],
            device,
        )

    def cross_arrives(group, n):
        first, count = GROUPS[group]
        ref = cross_in.at[n, pl.ds(1, G - 1), pl.ds(first * 2 * E, count * 2 * E)]
        return remote(ref, ref, z_s.at[0], z_r.at[group, n], partner)

    def loop(count, body):
        def run(i, carry):
            body(i)
            return carry

        lax.fori_loop(0, count, run, 0)

    load_a.wait()
    for load in (load_p, load_m):
        load.start()

    def arrange(n):
        columns = pl.ds(pl.multiple_of(n * W, W), W)
        value = raw[:, columns].astype(F32)
        pieces = []
        for i in range(CHUNKS):
            for part in range(2):
                for block in range(G):
                    start = part * H + block * T + i * E
                    pieces.append(value[start : start + E])
        ordered = jnp.concatenate(pieces, axis=0).astype(BF)
        mine[:, columns] = ordered

        @pl.when(end)
        def _():
            panel[yh, :, pl.ds(pl.multiple_of(core * D + n * W, W), W)] = ordered

    loop(CHUNKS, arrange)
    pl.semaphore_wait(barrier, 6 + G - 1)

    @pl.when(end)
    def _():
        loop(CHUNKS, lambda i: t_end(i).start())
        loop(CHUNKS, lambda i: share(yh, i).start())

    @pl.when(jnp.logical_not(end))
    def _():
        loop(CHUNKS, lambda i: t_far(i).start())
        loop(CHUNKS, lambda i: t_middle(i).start())

    for load in (load_p, load_m):
        load.wait()
    first = jnp.broadcast_to(bubble[0:1, :].astype(F32), (W, H)).T
    second = jnp.broadcast_to(bubble[1:2, :].astype(F32), (W, H)).T

    def make_bubbled(n):
        columns = pl.ds(pl.multiple_of(n * W, W), W)
        real = prev[pl.ds(0, H), columns].astype(F32)
        imag = prev[pl.ds(H, H), columns].astype(F32)
        rows = pl.ds(pl.multiple_of(x * H, H), H)
        bub[n, rows, pl.ds(0, W)] = (first * real - second * imag).astype(BF)
        bub[n, rows, pl.ds(W, W)] = (first * imag + second * real).astype(BF)

    def send_bubbled(n):
        for way in (0, 1):
            bx(n, way).start()

    def first_bubbled(n):
        make_bubbled(n)
        send_bubbled(n)

    loop(AHEAD, first_bubbled)
    loop(CHUNKS - AHEAD, lambda n: make_bubbled(n + AHEAD))

    goes = []
    for step in range(G):
        target = lax.rem(z + step, G)
        index = jnp.int32(0)
        for block in range(G):
            index = jnp.where(cmap[target, row * G + block] == z, block, index)
        goes.append(index)
    comes = []
    for block in range(G):
        back = z - cmap[z, row * G + block]
        comes.append(jnp.where(back < 0, back + G, back))

    def product(group, n, slot, target):
        first, count = GROUPS[group]
        rows = group_rows(group)
        total = jnp.dot(panel[slot, rows], bub[n], preferred_element_type=F32)
        mid = W // 2
        for i in range(count):
            upper = total[i * W : i * W + mid]
            lower = total[i * W + mid : i * W + W]
            start = (first + i) * W
            target[n, pl.ds(start, mid)] = (upper[:, :W] - lower[:, W:]).astype(target.dtype)
            target[n, pl.ds(start + mid, mid)] = (upper[:, W:] + lower[:, :W]).astype(target.dtype)

    def multiply(group, n):
        product(group, n, other, part_out)
        product(group, n, yh, kept)
        if group == 2:
            c(group, n).start()
        else:

            @pl.when(jnp.logical_not(end) | (n >= HELD))
            def _():
                c(group, n).start()


    def finish(group, n):
        first, count = GROUPS[group]
        rows = group_rows(group)
        columns = pl.ds(pl.multiple_of(n * W, W), W)
        c(group, n).wait_recv()
        value = mine[rows, columns].astype(F32) + (kept[n, rows] + part_in[n, rows].astype(F32))
        kept[n, rows] = value
        high = pl.ds(first * 2 * E, count * 2 * E)
        for block in range(G):
            pieces = []
            for i in range(count):
                for part in range(2):
                    start = i * W + part * (W // 2) + block * E
                    pieces.append(value[start : start + E])
            turn[block, high] = jnp.concatenate(pieces, axis=0).astype(BF)
        for step in FAR_FIRST:
            if step:
                cross_out[n, step, high] = turn[goes[step], high]
                cross(group, n, step).start()
            else:
                cross_in[n, step, high] = turn[goes[step], high]

    def store(which, n):
        columns = pl.ds(pl.multiple_of(n * W, W), W)
        source = (updated, crossed)[which].at[:, columns]
        return pltpu.make_async_copy(source, (updated_out, crossed_out)[which].at[:, columns], store_sem.at[which])

    def write(n):
        columns = pl.ds(pl.multiple_of(n * W, W), W)
        value = kept[n]
        for part in range(2):
            pieces = []
            for block in range(G):
                for i in range(CHUNKS):
                    start = i * W + part * (W // 2) + block * E
                    pieces.append(value[start : start + E])
            updated[pl.ds(part * H, H), columns] = jnp.concatenate(pieces, axis=0).astype(BF)
        store(0, n).start()

    def place(n):
        columns = pl.ds(pl.multiple_of(n * W, W), W)
        for group in (0, 1, 2):
            cross_arrives(group, n).wait_recv()
        settled[...] = cross_in[n]
        blocks = [settled[comes[block]].astype(F32) for block in range(G)]
        for part in range(2):
            pieces = []
            for block in range(G):
                for i in range(CHUNKS):
                    start = i * 2 * E + part * E
                    pieces.append(blocks[block][start : start + E])
            crossed[pl.ds(part * H, H), columns] = jnp.concatenate(pieces, axis=0).astype(BF)
        store(1, n).start()

    def relay_bubbled(n):
        for way in (0, 1):
            bx_arrives(n, way).wait_recv()
            by(n, way).start()

        @pl.when(n + AHEAD < CHUNKS)
        def _():
            send_bubbled(n + AHEAD)

    def group_arrives(group):
        share_arrives(yh, group).wait_recv()
        share_arrives(other, group).wait_recv()

    def bubbled_arrives(n):
        for way in (0, 1):
            by_arrives(n, way).wait_recv()

    def early(n):
        bubbled_arrives(n)
        multiply(0, n)
        multiply(1, n)

    def sent(ref, semaphore):
        remote(ref, ref, semaphore, load_sem.at[0], partner).wait_send()

    def pass_on(i):
        @pl.when(jnp.logical_not(end))
        def _():
            t1_arrives(i).wait_recv()
            share(yh, i).start()

        t2_arrives(i).wait_recv()
        share(other, i).start()

    def release():
        @pl.when(end)
        def _():
            pl.semaphore_wait(go, 1)

            def start(n):
                c(0, n).start()
                c(1, n).start()

            loop(HELD, start)

        @pl.when(jnp.logical_not(end))
        def _():
            sent(mine, t_s.at[0])
            pl.semaphore_signal(go, inc=1, device_id=beside, device_id_type=MESH)

    def gather(i):
        @pl.when(i == CHUNKS - 1)
        def _():
            release()

        pass_on(i)

        @pl.when((i < 2) | (i == 3) | (i == 4) | (i == 6))
        def _():
            relay_bubbled(jnp.where(i < 2, i, jnp.where(i < 5, i - 1, 4)))

        @pl.when(i == CHUNKS - 1)
        def _():
            finish(0, 0)

        @pl.when(i == 4)
        def _():
            group_arrives(0)
            group_arrives(1)
            early(0)

        @pl.when(i >= 4)
        def _():
            early(i - 3)

    loop(CHUNKS, gather)
    finish(1, 0)
    group_arrives(2)

    def step(t):
        late = jnp.where(t == 2, 4, jnp.where(t == 5, 5, 6))
        zero = (t < 3) | (t == 7) | (t == 9) | (t == 11)

        @pl.when((t == 5) | (t == 6))
        def _():
            early(late)
            multiply(2, late)

        @pl.when(t < 3)
        def _():
            multiply(2, t)

        @pl.when((t == 1) | (t == 3))
        def _():
            relay_bubbled(jnp.where(t == 1, 5, 6))

        @pl.when(zero)
        def _():
            n = jnp.where(t < 3, t + 1, (t + 1) // 2)
            finish(0, n)
            finish(1, n)

        @pl.when(t == 2)
        def _():
            multiply(2, 3)
            early(4)
            multiply(2, 4)

        @pl.when(jnp.logical_not(zero) & (t < 13))
        def _():
            n = jnp.where(t < 7, t - 3, t // 2)
            finish(2, n)
            write(n)

        @pl.when(t >= 10)
        def _():
            place(t - 10)

    loop(CHUNKS + 10, step)

    @pl.when(end)
    def _():
        sent(mine, t_s.at[0])

    @pl.when(jnp.logical_not(end))
    def _():
        sent(mine, t_s.at[1])

    sent(panel.at[:, :, half(core)], d_s.at[0])
    for way in (0, 1):
        sent(bub.at[:, pl.ds(pl.multiple_of(x * H, H), H)], bx_s.at[way])
        start = lax.rem(x + (3, 1)[way], 4) * H + way * (H // 2)
        sent(bub.at[:, pl.ds(pl.multiple_of(start, H // 2), H // 2)], by_s.at[way])
    sent(part_out, c_s.at[0])
    sent(cross_out.at[:, pl.ds(1, G - 1)], z_s.at[0])
    for which in (0, 1):
        source, target = ((updated, updated_out), (crossed, crossed_out))[which]
        pltpu.make_async_copy(source, target, store_sem.at[which]).wait()


def hand_over(updated, crossed, updated_out, crossed_out, sem):
    copies = [
        pltpu.make_async_copy(updated, updated_out, sem.at[0]),
        pltpu.make_async_copy(crossed, crossed_out, sem.at[1]),
    ]
    for copy in copies:
        copy.start()
    for copy in copies:
        copy.wait()


def shards(vertex, bubble, previous, cross_map):
    dma = pltpu.SemaphoreType.DMA
    updated, crossed = pl.pallas_call(
        kernel,
        out_shape=[pltpu.VMEM((D, D), BF)] * 2,
        in_specs=[
            pl.BlockSpec(memory_space=pltpu.HBM),
            pl.BlockSpec(memory_space=pltpu.VMEM),
            pl.BlockSpec(memory_space=pltpu.HBM),
            pl.BlockSpec(memory_space=pltpu.HBM),
        ],
        out_specs=[pl.BlockSpec(memory_space=pl.ANY)] * 2,
        scratch_shapes=[
            pltpu.VMEM((D, D), BF),
            pltpu.VMEM((D, D), BF),
            pltpu.VMEM((2, D, 2 * D), BF),
            pltpu.VMEM((D, D), BF),
            pltpu.VMEM((D, D), BF),
            pltpu.VMEM((D, D), BF),
            pltpu.SMEM((G, G * G), jnp.int32),
            pltpu.VMEM((CHUNKS, 4 * H, 2 * W), BF),
            pltpu.VMEM((CHUNKS, D, W), F32),
            pltpu.VMEM((CHUNKS, D, W), BF),
            pltpu.VMEM((CHUNKS, D, W), BF),
            pltpu.VMEM((G, 2 * T, W), BF),
            pltpu.VMEM((G, 2 * T, W), BF),
            pltpu.VMEM((CHUNKS, G, 2 * T, W), BF),
            pltpu.VMEM((CHUNKS, G, 2 * T, W), BF),
            dma((3,)),
            dma((2,)),
            dma((2,)),
            dma((CHUNKS,)),
            dma((CHUNKS,)),
            dma((1,)),
            dma((2, 3)),
            dma((2,)),
            dma((2, CHUNKS)),
            dma((2,)),
            dma((2, CHUNKS)),
            dma((1,)),
            dma((3, CHUNKS)),
            dma((1,)),
            dma((3, CHUNKS)),
            pltpu.SemaphoreType.REGULAR,
        ],
        compiler_params=pltpu.CompilerParams(
            collective_id=0, has_side_effects=True, vmem_limit_bytes=60 * 2**20
        ),
        cost_estimate=pl.CostEstimate(flops=8 * H * 4 * D * D, bytes_accessed=8 * D * D, transcendentals=0),
    )(vertex.reshape(D, D), bubble.reshape(2, H), previous.reshape(D, D), cross_map)
    updated, crossed = pl.pallas_call(
        hand_over,
        out_shape=[jax.ShapeDtypeStruct((D, D), BF)] * 2,
        in_specs=[pl.BlockSpec(memory_space=pl.ANY)] * 2,
        out_specs=[pl.BlockSpec(memory_space=pl.ANY)] * 2,
        scratch_shapes=[pltpu.SemaphoreType.DMA((2,))],
        compiler_params=pltpu.CompilerParams(vmem_limit_bytes=4 * 2**20),
        cost_estimate=pl.CostEstimate(flops=0, bytes_accessed=8 * D * D, transcendentals=0),
    )(updated, crossed)
    return updated.reshape(1, 2, H, D), crossed.reshape(1, 2, H, D)


def solution(mesh):
    in_specs = (
        P("xfer", None, "row", "col"),
        P("xfer", None, "row"),
        P("xfer", None, "row", "col"),
        P(),
    )
    out_specs = (P("xfer", None, "row", "col"), P("xfer", None, "row", "col"))
    return jax.shard_map(shards, mesh=mesh, in_specs=in_specs, out_specs=out_specs, check_vma=False)
```

```python
import jax
import jax.numpy as jnp
from jax import lax
from jax.experimental import pallas as pl
from jax.experimental.pallas import tpu as pltpu
from jax.sharding import PartitionSpec as P

MESH = pl.DeviceIdType.MESH
CHUNKS = 7
W = 128
H = 448
D = 896
G = 8
T = 56
HELD = 3
FAR_FIRST = (4, 3, 5, 2, 6, 1, 7, 0)
AHEAD = 2
E = 8
GROUPS = ((0, 2), (2, 2), (4, 3))
BF = jnp.bfloat16
F32 = jnp.float32


def kernel(
    vertex,
    bubble,
    previous,
    cross_map,
    updated_out,
    crossed_out,
    updated,
    crossed,
    panel,
    mine,
    raw,
    prev,
    diag,
    cmap,
    bub,
    kept,
    part_out,
    part_in,
    turn,
    settled,
    cross_out,
    cross_in,
    load_sem,
    store_sem,
    t_s,
    t1_r,
    t2_r,
    d_s,
    d_r,
    bx_s,
    bx_r,
    by_s,
    by_r,
    c_s,
    c_r,
    z_s,
    z_r,
    go,
):
    z = lax.axis_index("xfer")
    row = lax.axis_index("row")
    col = lax.axis_index("col")
    x = lax.rem(row, 4)
    yh = lax.div(row, 4)
    yl = lax.div(col, 2)
    core = lax.rem(col, 2)
    other = 1 - yh
    right = (z, yh * 4 + lax.rem(x + 1, 4), col)
    left = (z, yh * 4 + lax.rem(x + 3, 4), col)
    beside = (z, row, (1 - yl) * 2 + core)
    across = (z, other * 4 + x, (1 - yl) * 2 + core)
    sibling = (z, row, yl * 2 + 1 - core)
    partner = (z, other * 4 + x, col)
    end = yh == yl

    def remote(src, dst, send, recv, device):
        return pltpu.make_async_remote_copy(
            src_ref=src, dst_ref=dst, send_sem=send, recv_sem=recv, device_id=device, device_id_type=MESH
        )

    load_a = pltpu.make_async_copy(vertex, raw, load_sem.at[0])
    load_p = pltpu.make_async_copy(previous, prev, load_sem.at[1])
    load_d = pltpu.make_async_copy(bubble, diag, load_sem.at[2])
    load_m = pltpu.make_async_copy(cross_map, cmap, load_sem.at[3])
    load_a.start()

    barrier = pltpu.get_barrier_semaphore()
    for step in FAR_FIRST[:-1]:
        pl.semaphore_signal(barrier, inc=1, device_id=(lax.rem(z + step, G), row, col), device_id_type=MESH)
    for device in (right, left, beside, across, sibling, partner):
        pl.semaphore_signal(barrier, inc=1, device_id=device, device_id_type=MESH)


    def half(which):
        return pl.ds(pl.multiple_of(which * D, D), D)

    def row_chunk(i):
        return pl.ds(pl.multiple_of(i * W, W), W)

    def t_end(i):
        rows = row_chunk(i)
        return remote(mine.at[rows], panel.at[yh, rows, half(core)], t_s.at[0], t1_r.at[i], beside)

    def t_middle(i):
        rows = row_chunk(i)
        return remote(mine.at[rows], panel.at[yh, rows, half(core)], t_s.at[0], t2_r.at[i], across)

    def t_far(i):
        rows = row_chunk(i)
        return remote(mine.at[rows], panel.at[yh, rows, half(core)], t_s.at[1], t2_r.at[i], partner)

    def t1_arrives(i):
        ref = panel.at[yh, row_chunk(i), half(core)]
        return remote(ref, ref, t_s.at[0], t1_r.at[i], beside)

    def t2_arrives(i):
        ref = panel.at[other, row_chunk(i), half(core)]
        return remote(ref, ref, t_s.at[0], t2_r.at[i], across)

    def group_of(i):
        return jnp.where(i < GROUPS[1][0], 0, jnp.where(i < GROUPS[2][0], 1, 2))

    def group_rows(group):
        first, count = GROUPS[group]
        return pl.ds(first * W, count * W)

    def share(slot, i):
        ref = panel.at[slot, row_chunk(i), half(core)]
        return remote(ref, ref, d_s.at[0], d_r.at[jnp.where(slot == yh, 0, 1), group_of(i)], sibling)

    def share_arrives(slot, group):
        ref = panel.at[slot, group_rows(group), half(1 - core)]
        return remote(ref, ref, d_s.at[0], d_r.at[jnp.where(slot == yh, 0, 1), group], sibling)

    def bx(n, way):
        ref = bub.at[n, pl.ds(pl.multiple_of(x * H, H), H)]
        return remote(ref, ref, bx_s.at[way], bx_r.at[way, n], (right, left)[way])

    def bx_arrives(n, way):
        ref = bub.at[n, pl.ds(pl.multiple_of(lax.rem(x + (3, 1)[way], 4) * H, H), H)]
        return remote(ref, ref, bx_s.at[way], bx_r.at[way, n], (right, left)[way])

    def by(n, way):
        start = lax.rem(x + (3, 1)[way], 4) * H + way * (H // 2)
        ref = bub.at[n, pl.ds(pl.multiple_of(start, H // 2), H // 2)]
        return remote(ref, ref, by_s.at[way], by_r.at[way, n], (right, left)[way])

    def by_arrives(n, way):
        start = lax.rem(x + 2, 4) * H + way * (H // 2)
        ref = bub.at[n, pl.ds(pl.multiple_of(start, H // 2), H // 2)]
        return remote(ref, ref, by_s.at[way], by_r.at[way, n], (right, left)[way])

    def c(group, n):
        rows = group_rows(group)
        return remote(part_out.at[n, rows], part_in.at[n, rows], c_s.at[0], c_r.at[group, n], partner)

    def cross(group, n, step):
        first, count = GROUPS[group]
        rows = pl.ds(first * 2 * E, count * 2 * E)
        device = (lax.rem(z + step, G), row, col)
        return remote(
            cross_out.at[n, step, rows],
            cross_in.at[n, step, rows],
            z_s.at[0],
            z_r.at[group, n],
            device,
        )

    def cross_arrives(group, n):
        first, count = GROUPS[group]
        ref = cross_in.at[n, pl.ds(1, G - 1), pl.ds(first * 2 * E, count * 2 * E)]
        return remote(ref, ref, z_s.at[0], z_r.at[group, n], partner)

    def loop(count, body):
        def run(i, carry):
            body(i)
            return carry

        lax.fori_loop(0, count, run, 0)

    load_a.wait()
    for load in (load_p, load_d, load_m):
        load.start()

    def arrange(n):
        columns = pl.ds(pl.multiple_of(n * W, W), W)
        value = raw[:, columns].astype(F32)
        pieces = []
        for i in range(CHUNKS):
            for part in range(2):
                for block in range(G):
                    start = part * H + block * T + i * E
                    pieces.append(value[start : start + E])
        ordered = jnp.concatenate(pieces, axis=0).astype(BF)
        mine[:, columns] = ordered

        @pl.when(end)
        def _():
            panel[yh, :, pl.ds(pl.multiple_of(core * D + n * W, W), W)] = ordered

    loop(CHUNKS, arrange)
    pl.semaphore_wait(barrier, 6 + G - 1)

    @pl.when(end)
    def _():
        loop(CHUNKS, lambda i: t_end(i).start())
        loop(CHUNKS, lambda i: share(yh, i).start())

    @pl.when(jnp.logical_not(end))
    def _():
        loop(CHUNKS, lambda i: t_middle(i).start())
        loop(CHUNKS, lambda i: t_far(i).start())

    for load in (load_p, load_d, load_m):
        load.wait()
    first = jnp.broadcast_to(diag[0:1, :].astype(F32), (W, H)).T
    second = jnp.broadcast_to(diag[1:2, :].astype(F32), (W, H)).T

    def make_bubbled(n):
        columns = pl.ds(pl.multiple_of(n * W, W), W)
        real = prev[pl.ds(0, H), columns].astype(F32)
        imag = prev[pl.ds(H, H), columns].astype(F32)
        rows = pl.ds(pl.multiple_of(x * H, H), H)
        bub[n, rows, pl.ds(0, W)] = (first * real - second * imag).astype(BF)
        bub[n, rows, pl.ds(W, W)] = (first * imag + second * real).astype(BF)

    def send_bubbled(n):
        for way in (0, 1):
            bx(n, way).start()

    def first_bubbled(n):
        make_bubbled(n)
        send_bubbled(n)

    loop(AHEAD, first_bubbled)
    loop(CHUNKS - AHEAD, lambda n: make_bubbled(n + AHEAD))

    goes = []
    for step in range(G):
        target = lax.rem(z + step, G)
        index = jnp.int32(0)
        for block in range(G):
            index = jnp.where(cmap[target, row * G + block] == z, block, index)
        goes.append(index)
    comes = []
    for block in range(G):
        back = z - cmap[z, row * G + block]
        comes.append(jnp.where(back < 0, back + G, back))

    def product(group, n, slot, target):
        first, count = GROUPS[group]
        rows = group_rows(group)
        total = jnp.dot(panel[slot, rows], bub[n], preferred_element_type=F32)
        mid = W // 2
        for i in range(count):
            upper = total[i * W : i * W + mid]
            lower = total[i * W + mid : i * W + W]
            start = (first + i) * W
            target[n, pl.ds(start, mid)] = (upper[:, :W] - lower[:, W:]).astype(target.dtype)
            target[n, pl.ds(start + mid, mid)] = (upper[:, W:] + lower[:, :W]).astype(target.dtype)

    def multiply(group, n):
        product(group, n, other, part_out)
        product(group, n, yh, kept)
        if group == 2:
            c(group, n).start()
        else:

            @pl.when(jnp.logical_not(end) | (n >= HELD))
            def _():
                c(group, n).start()


    def finish(group, n):
        first, count = GROUPS[group]
        rows = group_rows(group)
        columns = pl.ds(pl.multiple_of(n * W, W), W)
        c(group, n).wait_recv()
        value = mine[rows, columns].astype(F32) + (kept[n, rows] + part_in[n, rows].astype(F32))
        kept[n, rows] = value
        high = pl.ds(first * 2 * E, count * 2 * E)
        for block in range(G):
            pieces = []
            for i in range(count):
                for part in range(2):
                    start = i * W + part * (W // 2) + block * E
                    pieces.append(value[start : start + E])
            turn[block, high] = jnp.concatenate(pieces, axis=0).astype(BF)
        for step in FAR_FIRST:
            if step:
                cross_out[n, step, high] = turn[goes[step], high]
                cross(group, n, step).start()
            else:
                cross_in[n, step, high] = turn[goes[step], high]

    def store(which, n):
        columns = pl.ds(pl.multiple_of(n * W, W), W)
        source = (updated, crossed)[which].at[:, columns]
        return pltpu.make_async_copy(source, (updated_out, crossed_out)[which].at[:, columns], store_sem.at[which])

    def write(n):
        columns = pl.ds(pl.multiple_of(n * W, W), W)
        value = kept[n]
        for part in range(2):
            pieces = []
            for block in range(G):
                for i in range(CHUNKS):
                    start = i * W + part * (W // 2) + block * E
                    pieces.append(value[start : start + E])
            updated[pl.ds(part * H, H), columns] = jnp.concatenate(pieces, axis=0).astype(BF)
        store(0, n).start()

    def place(n):
        columns = pl.ds(pl.multiple_of(n * W, W), W)
        for group in (0, 1, 2):
            cross_arrives(group, n).wait_recv()
        settled[...] = cross_in[n]
        blocks = [settled[comes[block]].astype(F32) for block in range(G)]
        for part in range(2):
            pieces = []
            for block in range(G):
                for i in range(CHUNKS):
                    start = i * 2 * E + part * E
                    pieces.append(blocks[block][start : start + E])
            crossed[pl.ds(part * H, H), columns] = jnp.concatenate(pieces, axis=0).astype(BF)
        store(1, n).start()

    def relay_bubbled(n):
        for way in (0, 1):
            bx_arrives(n, way).wait_recv()
            by(n, way).start()

        @pl.when(n + AHEAD < CHUNKS)
        def _():
            send_bubbled(n + AHEAD)

    def group_arrives(group):
        share_arrives(yh, group).wait_recv()
        share_arrives(other, group).wait_recv()

    def bubbled_arrives(n):
        for way in (0, 1):
            by_arrives(n, way).wait_recv()

    def early(n):
        bubbled_arrives(n)
        multiply(0, n)
        multiply(1, n)

    def sent(ref, semaphore):
        remote(ref, ref, semaphore, load_sem.at[0], partner).wait_send()

    def pass_on(i):
        @pl.when(jnp.logical_not(end))
        def _():
            t1_arrives(i).wait_recv()
            share(yh, i).start()

        t2_arrives(i).wait_recv()
        share(other, i).start()

    def release():
        @pl.when(end)
        def _():
            pl.semaphore_wait(go, 1)

            def start(n):
                c(0, n).start()
                c(1, n).start()

            loop(HELD, start)

        @pl.when(jnp.logical_not(end))
        def _():
            sent(mine, t_s.at[0])
            pl.semaphore_signal(go, inc=1, device_id=beside, device_id_type=MESH)

    def gather(i):
        @pl.when(i == CHUNKS - 1)
        def _():
            release()

        pass_on(i)

        @pl.when((i < 2) | (i == 3) | (i == 4) | (i == 6))
        def _():
            relay_bubbled(jnp.where(i < 2, i, jnp.where(i < 5, i - 1, 4)))

        @pl.when(i == CHUNKS - 1)
        def _():
            finish(0, 0)

        @pl.when(i == 4)
        def _():
            group_arrives(0)
            group_arrives(1)
            early(0)

        @pl.when(i >= 4)
        def _():
            early(i - 3)

    loop(CHUNKS, gather)
    finish(1, 0)
    group_arrives(2)

    def step(t):
        late = jnp.where(t == 2, 4, jnp.where(t == 5, 5, 6))
        zero = (t < 3) | (t == 7) | (t == 9) | (t == 11)

        @pl.when((t == 5) | (t == 6))
        def _():
            early(late)
            multiply(2, late)

        @pl.when(t < 3)
        def _():
            multiply(2, t)

        @pl.when((t == 1) | (t == 3))
        def _():
            relay_bubbled(jnp.where(t == 1, 5, 6))

        @pl.when(zero)
        def _():
            n = jnp.where(t < 3, t + 1, (t + 1) // 2)
            finish(0, n)
            finish(1, n)

        @pl.when(t == 2)
        def _():
            multiply(2, 3)
            early(4)
            multiply(2, 4)

        @pl.when(jnp.logical_not(zero) & (t < 13))
        def _():
            n = jnp.where(t < 7, t - 3, t // 2)
            finish(2, n)
            write(n)

        @pl.when(t >= 10)
        def _():
            place(t - 10)

    loop(CHUNKS + 10, step)

    @pl.when(end)
    def _():
        sent(mine, t_s.at[0])

    @pl.when(jnp.logical_not(end))
    def _():
        sent(mine, t_s.at[1])

    sent(panel.at[:, :, half(core)], d_s.at[0])
    for way in (0, 1):
        sent(bub.at[:, pl.ds(pl.multiple_of(x * H, H), H)], bx_s.at[way])
        start = lax.rem(x + (3, 1)[way], 4) * H + way * (H // 2)
        sent(bub.at[:, pl.ds(pl.multiple_of(start, H // 2), H // 2)], by_s.at[way])
    sent(part_out, c_s.at[0])
    sent(cross_out.at[:, pl.ds(1, G - 1)], z_s.at[0])
    for which in (0, 1):
        source, target = ((updated, updated_out), (crossed, crossed_out))[which]
        pltpu.make_async_copy(source, target, store_sem.at[which]).wait()


def hand_over(updated, crossed, updated_out, crossed_out, sem):
    copies = [
        pltpu.make_async_copy(updated, updated_out, sem.at[0]),
        pltpu.make_async_copy(crossed, crossed_out, sem.at[1]),
    ]
    for copy in copies:
        copy.start()
    for copy in copies:
        copy.wait()


def shards(vertex, bubble, previous, cross_map):
    dma = pltpu.SemaphoreType.DMA
    updated, crossed = pl.pallas_call(
        kernel,
        out_shape=[pltpu.VMEM((D, D), BF)] * 2,
        in_specs=[
            pl.BlockSpec(memory_space=pltpu.HBM),
            pl.BlockSpec(memory_space=pltpu.HBM),
            pl.BlockSpec(memory_space=pltpu.HBM),
            pl.BlockSpec(memory_space=pltpu.HBM),
        ],
        out_specs=[pl.BlockSpec(memory_space=pl.ANY)] * 2,
        scratch_shapes=[
            pltpu.VMEM((D, D), BF),
            pltpu.VMEM((D, D), BF),
            pltpu.VMEM((2, D, 2 * D), BF),
            pltpu.VMEM((D, D), BF),
            pltpu.VMEM((D, D), BF),
            pltpu.VMEM((D, D), BF),
            pltpu.VMEM((2, H), BF),
            pltpu.SMEM((G, G * G), jnp.int32),
            pltpu.VMEM((CHUNKS, 4 * H, 2 * W), BF),
            pltpu.VMEM((CHUNKS, D, W), F32),
            pltpu.VMEM((CHUNKS, D, W), BF),
            pltpu.VMEM((CHUNKS, D, W), BF),
            pltpu.VMEM((G, 2 * T, W), BF),
            pltpu.VMEM((G, 2 * T, W), BF),
            pltpu.VMEM((CHUNKS, G, 2 * T, W), BF),
            pltpu.VMEM((CHUNKS, G, 2 * T, W), BF),
            dma((4,)),
            dma((2,)),
            dma((2,)),
            dma((CHUNKS,)),
            dma((CHUNKS,)),
            dma((1,)),
            dma((2, 3)),
            dma((2,)),
            dma((2, CHUNKS)),
            dma((2,)),
            dma((2, CHUNKS)),
            dma((1,)),
            dma((3, CHUNKS)),
            dma((1,)),
            dma((3, CHUNKS)),
            pltpu.SemaphoreType.REGULAR,
        ],
        compiler_params=pltpu.CompilerParams(
            collective_id=0, has_side_effects=True, vmem_limit_bytes=60 * 2**20
        ),
        cost_estimate=pl.CostEstimate(flops=8 * H * 4 * D * D, bytes_accessed=8 * D * D, transcendentals=0),
    )(vertex.reshape(D, D), bubble.reshape(2, H), previous.reshape(D, D), cross_map)
    updated, crossed = pl.pallas_call(
        hand_over,
        out_shape=[jax.ShapeDtypeStruct((D, D), BF)] * 2,
        in_specs=[pl.BlockSpec(memory_space=pl.ANY)] * 2,
        out_specs=[pl.BlockSpec(memory_space=pl.ANY)] * 2,
        scratch_shapes=[pltpu.SemaphoreType.DMA((2,))],
        compiler_params=pltpu.CompilerParams(vmem_limit_bytes=4 * 2**20),
        cost_estimate=pl.CostEstimate(flops=0, bytes_accessed=8 * D * D, transcendentals=0),
    )(updated, crossed)
    return updated.reshape(1, 2, H, D), crossed.reshape(1, 2, H, D)


def solution(mesh):
    in_specs = (
        P("xfer", None, "row", "col"),
        P("xfer", None, "row"),
        P("xfer", None, "row", "col"),
        P(),
    )
    out_specs = (P("xfer", None, "row", "col"), P("xfer", None, "row", "col"))
    return jax.shard_map(shards, mesh=mesh, in_specs=in_specs, out_specs=out_specs, check_vma=False)
```
